32 devices in a mesh: sec: 4 (over z), gen: 8 (over y, x, core).
Axes of the slice: x: 2, y: 2, z: 4, core: 2. Of those that a mesh axis runs over, the one named last changes fastest.
Arguments:
- amps_left: bfloat16 [32, 4096, 256], P('sec', 'gen'), may hold values from -2 to 2
- amps_right: bfloat16 [32, 4096, 256], P('sec', 'gen'), may hold values from -2 to 2
- block_sizes: int32 [32], P('sec'), may hold values from 1 to 256, 4096 in all
- slab: bfloat16 [256, 64, 4096], P('gen', None, 'sec'), may hold values from -0.01171875 to 0.01171875
- fcore: bfloat16 [256, 64], P('gen'), may hold values from -6 to 6
Outputs:
- rdm: bfloat16 [4096, 4096], P('gen', 'sec')
- grad: float32 [256, 64], P('gen')
The draws below stay inside these ranges and needn't reach their ends.
Inputs may be any that keep to these rules, and one draw needn't show every extreme that they name: block_sizes of all sectors sum to 4096, and some sector has exactly 256 live states.
All inputs are finite; a program needn't handle non-finite values. No bound on the sum of `block_sizes` on one device may be relied on, other than what follows from the above.
Results may differ from the reference program's by a relative error of at most 0.0029.
Values may be sent and summed in bfloat16 or wider, within the bound.
No kernel may reach another device: no remote copies, remote signals or barrier semaphores. Data moves between devices by JAX's collectives and lax.ppermute only.
A program may use at most 64 MiB of HBM per device.

```python
import math
import jax
import jax.numpy as jnp
import numpy as np
from jax import lax

NA = 64
NP = 4096
M = 256
SECTORS = 32
PG_DEV = 32
P_SIZE = 256


def level_of(stream_key, extent, cuts, smallest, top_value):
    factor_of, own = 1.0, jax.random.fold_in(stream_key, 6)
    for axis_at, parts in cuts:
        steps = jnp.exp(jax.random.uniform(jax.random.fold_in(own, axis_at), (parts,), jnp.float32, smallest / len(cuts), top_value / len(cuts)))
        factor_of = factor_of * jnp.repeat(steps, extent[axis_at] // parts).reshape([-1 if axis == axis_at else 1 for axis in range(len(extent))])
    return factor_of


def length_profile(count, total, most, skew):
    portions = [(1 << 20) // math.isqrt(rank ** skew) + 1 for rank in range(2, count + 1)]
    spare, given = total - most - (count - 1), [1] * (count - 1)
    while spare > 0:
        free = [i for i in range(count - 1) if given[i] < most]
        pool, left = sum([portions[i] for i in free]), spare
        for i in free:
            more = min(most - given[i], max(1, left * portions[i] // pool), spare)
            given[i] = given[i] + more
            spare = spare - more
    return np.array([most] + given)


def uneven_parts(key, amount, total, limit, lean):
    if amount == 2:
        one = jax.random.randint(key, (), max(1, total - limit), min(limit, total - 1) + 1)
        return jnp.stack([one, total - one])
    tallies = jnp.asarray(length_profile(amount, total, limit, lean), jnp.int32)
    pairs = (amount - 1) // 2
    donor, sink = tallies[1:1 + 2 * pairs:2], tallies[2:2 + 2 * pairs:2]
    margin = jnp.minimum(donor - 1, limit - sink)
    shifted = jax.random.randint(jax.random.fold_in(key, 1), (pairs,), 0, 1 << 20) % (margin + 1)
    tallies = tallies.at[1:1 + 2 * pairs:2].set(donor - shifted).at[2:2 + 2 * pairs:2].set(sink + shifted)
    return tallies[jax.random.permutation(jax.random.fold_in(key, 2), amount)]


def noise(stream_key, shape, spread, bound, split=(), held_as=jnp.bfloat16):
    values = spread * jax.random.normal(stream_key, shape, jnp.float32)
    if split:
        values = values * level_of(stream_key, shape, split, -0.22, 0.18)
    return jnp.clip(values, -bound, bound).astype(held_as)


def setup_inputs(seed: int = 0) -> dict:
    seeds = jax.random.split(jax.random.key(seed), 6)
    return {
        "amps_left": noise(seeds[0], (SECTORS, NP, M), ((SECTORS * M // 2) ** -0.25), 2.0, ((0, 4), (1, 8))),
        "amps_right": noise(seeds[1], (SECTORS, NP, M), ((SECTORS * M // 2) ** -0.25), 2.0, ((0, 4), (1, 8))),
        "block_sizes": uneven_parts(seeds[2], SECTORS, SECTORS * M // 2, M, 2).astype(jnp.int32),
        "slab": noise(seeds[3], (P_SIZE, NA, NP), (NA * NP) ** -0.5, 0.01171875, ((0, 8), (2, 4))),
        "fcore": noise(seeds[4], (P_SIZE, NA), 1.0, 6.0, ((0, 8),)),
    }


def reference(amps_left, amps_right, block_sizes, slab, fcore):
    live = (jnp.arange(M, dtype=jnp.int32)[None, :] < block_sizes[:, None]).astype(jnp.float32)
    left = amps_left.astype(jnp.float32) * live[:, None, :]
    right = amps_right.astype(jnp.float32)
    pairs = jnp.einsum("srm,sqm->rq", left, right, precision=lax.Precision.HIGHEST)
    rdm = pairs.astype(jnp.bfloat16)
    whole = rdm.astype(jnp.float32)
    four = whole.reshape(NA, NA, NA, NA)
    one = jnp.einsum("utvv->ut", four) / NA
    three = whole.reshape(NA, NA, NP)
    blocks = slab.reshape(P_SIZE // PG_DEV, PG_DEV, NA, NP)

    def contract(block):
        return jnp.einsum("puq,tuq->pt", block.astype(jnp.float32), three, precision=lax.Precision.HIGHEST)

    two_body = lax.map(contract, blocks).reshape(P_SIZE, NA)
    fock = jnp.dot(fcore.astype(jnp.float32), one, precision=lax.Precision.HIGHEST) + two_body
    flipped = jnp.concatenate([fock[:NA].T, jnp.zeros((P_SIZE - NA, NA), jnp.float32)], 0)
    grad = 2.0 * (fock - flipped)
    return rdm, grad
```

```python
import jax
import jax.numpy as jnp
from jax import lax
from jax.sharding import PartitionSpec as P

CHUNKS = 4


def shards(secs, gens, amps_left, amps_right, block_sizes, slab, fcore):
    sectors, rows, states = amps_left.shape
    general, width, pair_cols = slab.shape
    chips = gens // 2
    per_sec = chips // secs
    bits = chips.bit_length() - 1
    chunks = CHUNKS if rows % (32 * CHUNKS) == 0 else 1
    half = rows // chunks // 2
    z = lax.axis_index("sec")
    g = lax.axis_index("gen")
    chip, core = g // 2, g % 2

    def across(value, flip):
        return lax.ppermute(value, "gen", [(i, i ^ flip) for i in range(gens)])

    def along(value, flip):
        return lax.ppermute(value, "sec", [(i, i ^ flip) for i in range(secs)])

    def gather(value, order):
        held = value[None]
        for bit in order:
            held = jnp.concatenate([held, across(held, 2 << bit)], axis=0)
        return held

    def place(relative, order):
        return sum(((relative >> bit) & 1) << at for at, bit in enumerate(order))

    orders = (tuple(range(bits)), tuple(reversed(range(bits))))
    live = (jnp.arange(states, dtype=jnp.int32)[None, :] < block_sizes[:, None]).astype(jnp.bfloat16)

    left = jnp.concatenate([amps_left, across(amps_left, 1)], axis=1) * live[:, None, :]

    by_core = slab.reshape(general, width, per_sec, 2, rows)
    kept = lax.dynamic_index_in_dim(by_core, core, 3, keepdims=False)
    given = lax.dynamic_index_in_dim(by_core, 1 - core, 3, keepdims=False)
    integrals = jnp.concatenate([kept, across(given, 1)], axis=0)

    column_ids = (
        z * pair_cols
        + jnp.arange(per_sec, dtype=jnp.int32)[:, None] * (2 * rows)
        + core * rows
        + jnp.arange(rows, dtype=jnp.int32)[None, :]
    )
    diagonal = (column_ids // width == column_ids % width).astype(jnp.bfloat16)

    pieces = []
    two_body = jnp.zeros((2 * general, width), jnp.float32)
    traced = jnp.zeros((width, width), jnp.float32)
    for chunk in range(chunks):
        start = chunk * 2 * half
        blocks = [
            gather(amps_right[:, start + i * half : start + (i + 1) * half], orders[i])
            for i in range(2)
        ]

        def partial_for(dest):
            wanted = chip ^ (dest * per_sec + jnp.arange(per_sec, dtype=jnp.int32))
            found = [
                jnp.take(blocks[i], place(wanted, orders[i]), axis=0) for i in range(2)
            ]
            right = jnp.concatenate(found, axis=2)
            return jnp.einsum(
                "srm,csqm->rcq", left, right, preferred_element_type=jnp.float32
            )

        arrived = [
            along(partial_for(z ^ flip).astype(jnp.bfloat16), flip) for flip in range(1, secs)
        ]
        total = partial_for(z)
        for value in arrived:
            total = total + value.astype(jnp.float32)
        piece = total.astype(jnp.bfloat16)
        pieces.append(piece)

        columns = per_sec * 2 * half
        by_row = piece.reshape(2, rows // width, width, columns)
        halves = [gather(by_row[i], orders[i]) for i in range(2)]
        table = jnp.arange(chips, dtype=jnp.int32)
        halves[1] = halves[1][jnp.array([sum(((p >> b) & 1) << a for a, b in enumerate(orders[1])) for p in range(chips)])]
        every = jnp.stack(halves, axis=1).reshape(width, width, columns)
        part = integrals[:, :, :, start : start + 2 * half].reshape(2 * general, width, columns)
        two_body = two_body + jnp.einsum(
            "puq,tuq->pt", part, every, preferred_element_type=jnp.float32
        )
        traced = traced + jnp.einsum(
            "tuq,q->tu",
            every,
            diagonal[:, start : start + 2 * half].reshape(columns),
            preferred_element_type=jnp.float32,
        )

    def ordered(value, axis):
        shape = value.shape
        split = value.reshape(shape[:axis] + (gens, shape[axis] // gens) + shape[axis + 1 :])
        return jnp.take(split, g ^ jnp.arange(gens), axis=axis).reshape(shape)

    two_body = ordered(two_body, 1)
    one = ordered(traced, 0) / width
    both = jnp.concatenate([fcore, across(fcore, 1)], axis=0).astype(jnp.float32)
    mine = two_body + jnp.dot(both, one, precision=lax.Precision.HIGHEST)
    theirs = across(mine, 1)
    fock = mine[:general] + theirs[general:]
    partner = mine[general:] + theirs[:general]

    first = jnp.where(core == 0, fock, partner)
    second = jnp.where(core == 0, partner, fock)
    active = jnp.concatenate([first, second], axis=0)
    flipped = lax.dynamic_slice_in_dim(active.T, core * general, general, axis=0)
    part = 2.0 * (fock - jnp.where(g < 2, flipped, 0.0))
    parts = [part] + [along(part, flip) for flip in range(1, secs)]
    while len(parts) > 1:
        parts = [a + b for a, b in zip(parts[::2], parts[1::2])]
    grad = parts[0]

    own = jnp.concatenate([p[:rows] for p in pieces], axis=2)
    other = across(jnp.concatenate([p[rows:] for p in pieces], axis=2), 1)
    lower = jnp.where(core == 0, own, other)
    upper = jnp.where(core == 0, other, own)
    rdm = jnp.stack([lower, upper], axis=2).reshape(rows, pair_cols)
    return rdm, grad


def solution(mesh):
    secs, gens = mesh.shape["sec"], mesh.shape["gen"]
    placed = (
        P("sec", "gen", None),
        P("sec", "gen", None),
        P("sec"),
        P("gen", None, "sec"),
        P("gen", None),
    )
    return jax.shard_map(
        lambda *args: shards(secs, gens, *args),
        mesh=mesh,
        in_specs=placed,
        out_specs=(P("gen", "sec"), P("gen", None)),
        check_vma=False,
    )
```

```python
import jax
import jax.numpy as jnp
from jax import lax
from jax.experimental import pallas as pl
from jax.experimental.pallas import tpu as pltpu
from jax.sharding import PartitionSpec as P

CHUNKS = 4
NT = (((1,), (1,)), ((), ()))

def partial_kernel(info, left, partner, own, xs, ys, da, db, o1, o2, o3, o0, rhs):
    sectors, tile, states = left.shape
    cols = own.shape[1]
    half = cols // 2
    base = info[0]

    @pl.when(pl.program_id(0) == 0)
    def _():
        for r in range(4):
            at = pl.multiple_of((base ^ r) * cols, cols)
            for s in range(sectors):
                lanes = slice(s * states, (s + 1) * states)
                if r < 3:
                    rhs[pl.ds(at, cols), lanes] = (own, xs, ys)[r][s]
                else:
                    rhs[pl.ds(at, half), lanes] = da[s]
                    rhs[pl.ds(at + half, half), lanes] = db[s]

    ids = lax.broadcasted_iota(jnp.int32, (tile, states), 1)
    for c, ref in enumerate((left, partner)):
        lhs = jnp.concatenate(
            [jnp.where(ids < info[1 + s], ref[s].astype(jnp.float32), 0.0).astype(jnp.bfloat16) for s in range(sectors)], axis=1
        )
        out = lax.dot_general(lhs, rhs[...], NT, preferred_element_type=jnp.float32)
        o0[c] = out[:, :cols]
        for i, o in enumerate((o1, o2, o3)):
            o[c] = out[:, (i + 1) * cols : (i + 2) * cols].astype(jnp.bfloat16)

def partial_products(info, left, partner, right, chunk, chunks, xs, ys, da, db, tile=256):
    sectors, rows, states = left.shape
    cols = rows // chunks
    whole = lambda a: pl.BlockSpec(a.shape, lambda i, info: (0,) * a.ndim)
    rspec = pl.BlockSpec((sectors, tile, states), lambda i, info: (0, i, 0))
    ospec = pl.BlockSpec((2, tile, cols), lambda i, info: (0, i, 0))
    sd = lambda t: jax.ShapeDtypeStruct((2, rows, cols), t)
    return pl.pallas_call(
        partial_kernel,
        grid_spec=pltpu.PrefetchScalarGridSpec(
            num_scalar_prefetch=1, grid=(rows // tile,),
            in_specs=[rspec, rspec, pl.BlockSpec((sectors, cols, states), lambda i, info: (0, chunk, 0))] + [whole(a) for a in (xs, ys, da, db)],
            out_specs=[ospec] * 4,
            scratch_shapes=[pltpu.VMEM((4 * cols, sectors * states), jnp.bfloat16)],
        ),
        out_shape=[sd(jnp.bfloat16)] * 3 + [sd(jnp.float32)],
        compiler_params=pltpu.CompilerParams(vmem_limit_bytes=40 * 2**20),
        name="partial_products",
    )(info, left, partner, right, xs, ys, da, db)

def combine_kernel(o0, a, b, c, plain, turned):
    width = turned.shape[0]
    f = jnp.float32
    total = ((o0[...] + a[...].astype(f)) + (b[...].astype(f) + c[...].astype(f)))
    two, rows, cols = total.shape
    plain[...] = total.astype(jnp.bfloat16)
    turned[...] = jnp.swapaxes(total.reshape(two * rows // width, width, cols), 0, 1).astype(jnp.bfloat16)

def combine(o0, a, b, c, width):
    two, rows, cols = o0.shape
    return pl.pallas_call(
        combine_kernel,
        out_shape=[jax.ShapeDtypeStruct(o0.shape, jnp.bfloat16), jax.ShapeDtypeStruct((width, two * rows // width, cols), jnp.bfloat16)],
        compiler_params=pltpu.CompilerParams(vmem_limit_bytes=40 * 2**20),
        name="combine",
    )(o0, a, b, c)

def fock_kernel(slab, diag, own, xs, ys, ds, fock, traced):
    width, orbitals, cols = slab.shape
    acc = jnp.zeros((orbitals, width), jnp.float32)
    mark = diag[...]
    for u in range(width):
        g = jnp.concatenate([own[u], xs[u], ys[u], ds[u]], axis=0)
        lhs = jnp.concatenate([slab[u], mark], axis=0)
        out = lax.dot_general(lhs, g, NT, preferred_element_type=jnp.float32)
        acc += out[:orbitals]
        traced[u, :] = out[orbitals]
    fock[...] = acc

def fock_terms(slab, diag, own, xs, ys, ds, chunk):
    width, orbitals, _ = slab.shape
    cols = own.shape[2]
    whole = lambda a: pl.BlockSpec(a.shape, lambda i: (0,) * a.ndim)
    return pl.pallas_call(
        fock_kernel,
        grid=(1,),
        in_specs=[pl.BlockSpec((width, orbitals, cols), lambda i: (0, 0, chunk))]
        + [whole(a) for a in (diag, own, xs, ys, ds)],
        out_specs=[pl.BlockSpec((orbitals, width), lambda i: (0, 0)), pl.BlockSpec((width, width), lambda i: (0, 0))],
        out_shape=[jax.ShapeDtypeStruct((orbitals, width), jnp.float32), jax.ShapeDtypeStruct((width, width), jnp.float32)],
        compiler_params=pltpu.CompilerParams(vmem_limit_bytes=40 * 2**20),
        name="fock_terms",
    )(slab, diag, own, xs, ys, ds)

def turn_kernel(a, b, o):
    o[:, :a.shape[0]] = jnp.swapaxes(a[...].astype(jnp.float32), 0, 1).astype(jnp.bfloat16)
    o[:, a.shape[0]:] = jnp.swapaxes(b[...].astype(jnp.float32), 0, 1).astype(jnp.bfloat16)

def turn(a, b, cols):
    g, w, n = a.shape
    return pl.pallas_call(turn_kernel, grid=(n // cols,),
        in_specs=[pl.BlockSpec((g, w, cols), lambda i: (0, 0, i))] * 2,
        out_specs=pl.BlockSpec((w, 2 * g, cols), lambda i: (0, 0, i)),
        out_shape=jax.ShapeDtypeStruct((w, 2 * g, n), jnp.bfloat16),
        compiler_params=pltpu.CompilerParams(vmem_limit_bytes=40 * 2**20), name="turn")(a, b)


def after(value, *done):
    return lax.optimization_barrier((value, *done))[0]


def shards(secs, gens, amps_left, amps_right, block_sizes, slab, fcore):
    sectors, rows, states = amps_left.shape
    general, width, pair_cols = slab.shape
    cols = rows // CHUNKS
    half = cols // 2
    z = lax.axis_index("sec")
    g = lax.axis_index("gen")
    chip, core = g // 2, g % 2

    def across(value, flip):
        return lax.ppermute(value, "gen", [(i, i ^ flip) for i in range(gens)])

    def along(value, flip):
        return lax.ppermute(value, "sec", [(i, i ^ flip) for i in range(secs)])

    info = jnp.concatenate([(chip ^ z)[None].astype(jnp.int32), block_sizes])

    def bra(chunk, *done):
        return after(amps_right[:, chunk * cols : (chunk + 1) * cols], *done)

    def forward(xs, ys):
        return across(xs[:, :half], 4), across(ys[:, half:], 2)

    def products(chunk, xs, ys, da, db, *done):
        return partial_products(after(info, *done), amps_left, partner_left, amps_right, chunk, CHUNKS, xs, ys, da, db)

    sent = bra(0)
    xs, ys = across(sent, 2), across(sent, 4)
    partner_left = across(amps_left, 1)

    kept = lax.dynamic_slice(slab, (0, 0, core * rows), (general, width, rows))
    given = lax.dynamic_slice(slab, (0, 0, (1 - core) * rows), (general, width, rows))
    integrals = turn(kept, across(given, 1), cols)

    column_ids = z * pair_cols + core * rows + jnp.arange(rows, dtype=jnp.int32)
    diagonal = jnp.broadcast_to(
        (column_ids // width == column_ids % width).astype(jnp.bfloat16)[None], (16, rows)
    )

    sums, moved, plains, terms, gathered = [None] * CHUNKS, [None] * CHUNKS, [], [], []

    def finish(chunk, *done):
        part = after(sums[chunk], *done)
        plain, turned = combine(part, *moved[chunk], width)
        plains.append(plain)
        order.append(plain)
        gathered.append((turned, across(turned, 2), across(turned, 4), across(turned, 6)))

    def contract(chunk, *done):
        at = slice(chunk * cols, (chunk + 1) * cols)
        marks = after(diagonal[:, at], *done)
        terms.append(fock_terms(integrals, marks, *gathered[chunk], chunk))
        order.append(terms[-1][0])

    order = []
    ahead = {0: (xs, ys)}
    for chunk in range(CHUNKS):
        for later in (chunk, chunk + 1):
            if later < CHUNKS and later not in ahead:
                sent = bra(later, *ahead[later - 1], *order[-1:])
                ahead[later] = across(sent, 2), across(sent, 4)
        xs, ys = ahead[chunk]
        *out, own = products(chunk, xs, ys, *forward(xs, ys), *order[-1:])
        sums[chunk] = own
        moved[chunk] = [along(value, flip + 1) for flip, value in enumerate(out)]
        order.append(own)
        if chunk >= 1:
            finish(chunk - 1, own)
        if chunk >= 2:
            contract(chunk - 2, *order[-1:])
    contract(CHUNKS - 2, *order[-1:])
    finish(CHUNKS - 1, *order[-1:])
    contract(CHUNKS - 1)

    two_body = sum(t[0] for t in terms)
    traced = sum(t[1] for t in terms)

    def ordered(value):
        return jnp.take(value.reshape(value.shape[0], gens, -1), g ^ jnp.arange(gens), axis=1).reshape(value.shape)

    one = ordered(traced).T / width
    both = jnp.concatenate([fcore, across(fcore, 1)], axis=0).astype(jnp.float32)
    mine = ordered(two_body) + jnp.dot(both, one, precision=lax.Precision.HIGHEST)
    theirs = across(mine, 1)
    fock = mine[:general] + theirs[general:]
    partner = mine[general:] + theirs[:general]

    first = jnp.where(core == 0, fock, partner)
    second = jnp.where(core == 0, partner, fock)
    active = jnp.concatenate([first, second], axis=0)
    flipped = lax.dynamic_slice_in_dim(active.T, core * general, general, axis=0)
    part = 2.0 * (fock - jnp.where(g < 2, flipped, 0.0))
    parts = [part] + [along(part, flip) for flip in range(1, secs)]
    while len(parts) > 1:
        parts = [a + b for a, b in zip(parts[::2], parts[1::2])]
    grad = parts[0]

    own = jnp.concatenate([p[0] for p in plains], axis=1)
    other = across(jnp.concatenate([p[1] for p in plains], axis=1), 1)
    rdm = jnp.concatenate(
        [jnp.where(core == 0, own, other), jnp.where(core == 0, other, own)], axis=1
    )
    return rdm, grad


def general_shards(secs, gens, amps_left, amps_right, block_sizes, slab, fcore):
    sectors, rows, states = amps_left.shape
    general, width, pair_cols = slab.shape
    chips = gens // 2
    per_sec = chips // secs
    bits = chips.bit_length() - 1
    chunks = 1
    half = rows // chunks // 2
    z = lax.axis_index("sec")
    g = lax.axis_index("gen")
    chip, core = g // 2, g % 2

    def across(value, flip):
        return lax.ppermute(value, "gen", [(i, i ^ flip) for i in range(gens)])

    def along(value, flip):
        return lax.ppermute(value, "sec", [(i, i ^ flip) for i in range(secs)])

    def gather(value, order):
        held = value[None]
        for bit in order:
            held = jnp.concatenate([held, across(held, 2 << bit)], axis=0)
        return held

    def place(relative, order):
        return sum(((relative >> bit) & 1) << at for at, bit in enumerate(order))

    orders = (tuple(range(bits)), tuple(reversed(range(bits))))
    live = (jnp.arange(states, dtype=jnp.int32)[None, :] < block_sizes[:, None]).astype(jnp.bfloat16)

    left = jnp.concatenate([amps_left, across(amps_left, 1)], axis=1) * live[:, None, :]

    by_core = slab.reshape(general, width, per_sec, 2, rows)
    kept = lax.dynamic_index_in_dim(by_core, core, 3, keepdims=False)
    given = lax.dynamic_index_in_dim(by_core, 1 - core, 3, keepdims=False)
    integrals = jnp.concatenate([kept, across(given, 1)], axis=0)

    column_ids = (
        z * pair_cols
        + jnp.arange(per_sec, dtype=jnp.int32)[:, None] * (2 * rows)
        + core * rows
        + jnp.arange(rows, dtype=jnp.int32)[None, :]
    )
    diagonal = (column_ids // width == column_ids % width).astype(jnp.bfloat16)

    pieces = []
    two_body = jnp.zeros((2 * general, width), jnp.float32)
    traced = jnp.zeros((width, width), jnp.float32)
    for chunk in range(chunks):
        start = chunk * 2 * half
        blocks = [
            gather(amps_right[:, start + i * half : start + (i + 1) * half], orders[i])
            for i in range(2)
        ]

        def partial_for(dest):
            wanted = chip ^ (dest * per_sec + jnp.arange(per_sec, dtype=jnp.int32))
            found = [
                jnp.take(blocks[i], place(wanted, orders[i]), axis=0) for i in range(2)
            ]
            right = jnp.concatenate(found, axis=2)
            return jnp.einsum(
                "srm,csqm->rcq", left, right, preferred_element_type=jnp.float32
            )

        arrived = [
            along(partial_for(z ^ flip).astype(jnp.bfloat16), flip) for flip in range(1, secs)
        ]
        total = partial_for(z)
        for value in arrived:
            total = total + value.astype(jnp.float32)
        piece = total.astype(jnp.bfloat16)
        pieces.append(piece)

        columns = per_sec * 2 * half
        by_row = piece.reshape(2, rows // width, width, columns)
        halves = [gather(by_row[i], orders[i]) for i in range(2)]
        table = jnp.arange(chips, dtype=jnp.int32)
        halves[1] = halves[1][jnp.array([sum(((p >> b) & 1) << a for a, b in enumerate(orders[1])) for p in range(chips)])]
        every = jnp.stack(halves, axis=1).reshape(width, width, columns)
        part = integrals[:, :, :, start : start + 2 * half].reshape(2 * general, width, columns)
        two_body = two_body + jnp.einsum(
            "puq,tuq->pt", part, every, preferred_element_type=jnp.float32
        )
        traced = traced + jnp.einsum(
            "tuq,q->tu",
            every,
            diagonal[:, start : start + 2 * half].reshape(columns),
            preferred_element_type=jnp.float32,
        )

    def ordered(value, axis):
        shape = value.shape
        split = value.reshape(shape[:axis] + (gens, shape[axis] // gens) + shape[axis + 1 :])
        return jnp.take(split, g ^ jnp.arange(gens), axis=axis).reshape(shape)

    two_body = ordered(two_body, 1)
    one = ordered(traced, 0) / width
    both = jnp.concatenate([fcore, across(fcore, 1)], axis=0).astype(jnp.float32)
    mine = two_body + jnp.dot(both, one, precision=lax.Precision.HIGHEST)
    theirs = across(mine, 1)
    fock = mine[:general] + theirs[general:]
    partner = mine[general:] + theirs[:general]

    first = jnp.where(core == 0, fock, partner)
    second = jnp.where(core == 0, partner, fock)
    active = jnp.concatenate([first, second], axis=0)
    flipped = lax.dynamic_slice_in_dim(active.T, core * general, general, axis=0)
    part = 2.0 * (fock - jnp.where(g < 2, flipped, 0.0))
    parts = [part] + [along(part, flip) for flip in range(1, secs)]
    while len(parts) > 1:
        parts = [a + b for a, b in zip(parts[::2], parts[1::2])]
    grad = parts[0]

    own = jnp.concatenate([p[:rows] for p in pieces], axis=2)
    other = across(jnp.concatenate([p[rows:] for p in pieces], axis=2), 1)
    lower = jnp.where(core == 0, own, other)
    upper = jnp.where(core == 0, other, own)
    rdm = jnp.stack([lower, upper], axis=2).reshape(rows, pair_cols)
    return rdm, grad


def solution(mesh):
    secs, gens = mesh.shape["sec"], mesh.shape["gen"]
    placed = (
        P("sec", "gen", None),
        P("sec", "gen", None),
        P("sec"),
        P("gen", None, "sec"),
        P("gen", None),
    )
    def step(*args):
        rows, general, width = args[0].shape[1], args[3].shape[0], args[3].shape[1]
        fits = secs == 4 and gens == 8 and 2 * general == width and rows % (256 * CHUNKS // 2) == 0
        return (shards if fits else general_shards)(secs, gens, *args)

    return jax.shard_map(
        step,
        mesh=mesh,
        in_specs=placed,
        out_specs=(P("gen", "sec"), P("gen", None)),
        check_vma=False,
    )
```

```python
import functools

import jax
import jax.numpy as jnp
from jax import lax
from jax.experimental import pallas as pl
from jax.experimental.pallas import tpu as pltpu
from jax.sharding import PartitionSpec as P

CHUNKS = 4
GROUPS = ((0,), (1,), (2,), (3,))
ORDER = (
    "W0", "M0", "W1", "A1", "P0", "M1", "W2", "A2", "P1", "M2", "C0", "W3", "A3", "P2", "C1", "M3", "F0", "C2", "F1", "P3", "F2", "C3", "R", "F3",
)
LIMIT = 50 * 2**20
NT = (((1,), (1,)), ((), ()))
HBM = pl.BlockSpec(memory_space=pltpu.HBM)
VMEM = pl.BlockSpec(memory_space=pltpu.VMEM)
SMEM = pl.BlockSpec(memory_space=pltpu.SMEM)
PARAMS = pltpu.CompilerParams(vmem_limit_bytes=LIMIT)


def partial_kernel(cuts, info, left, partner, *refs):
    *pieces, near, own, far, bra, ket, bra_sem, ket_sem = refs
    sectors, rows, states = left.shape
    cols = own.shape[2]
    copies = []
    for n, (ref, index, start, r) in enumerate(cuts):
        piece = pieces[ref].at[index]
        at = pl.multiple_of((info[0] ^ r) * cols + start, 16)
        copies.append(pltpu.make_async_copy(piece, bra.at[:, pl.ds(at, piece.shape[1])], bra_sem.at[n]))
    kets = [
        pltpu.make_async_copy(ref, ket.at[c], ket_sem.at[c]) for c, ref in enumerate((left, partner))
    ]
    for copy in copies + kets:
        copy.start()
    for copy in copies:
        copy.wait()
    ids = lax.broadcasted_iota(jnp.int32, (rows, states), 1)
    for c in range(2):
        kets[c].wait()
        out = None
        for s in range(sectors):
            live = jnp.where(ids < info[1 + s], ket[c, s].astype(jnp.float32), 0.0)
            term = lax.dot_general(
                live.astype(jnp.bfloat16), bra[s], NT, preferred_element_type=jnp.float32
            )
            out = term if out is None else out + term
        blocks = [out[:, k * cols : (k + 1) * cols] for k in range(4)]
        own[c] = blocks[0]
        near[0, c] = blocks[1].astype(jnp.bfloat16)
        near[1, c] = blocks[3].astype(jnp.bfloat16)
        far[c] = blocks[2].astype(far.dtype)


def partial_products(info, left, partner, cols, cuts, *pieces):
    sectors, rows, states = left.shape

    block = (2, rows, cols)
    return pl.pallas_call(
        functools.partial(partial_kernel, cuts),
        in_specs=[SMEM] + [HBM] * (2 + len(pieces)),
        out_specs=[VMEM] * 3,
        scratch_shapes=[
            pltpu.VMEM((sectors, 4 * cols, states), jnp.bfloat16),
            pltpu.VMEM((2, sectors, rows, states), jnp.bfloat16),
            pltpu.SemaphoreType.DMA((len(cuts),)),
            pltpu.SemaphoreType.DMA((2,)),
        ],
        out_shape=[
            jax.ShapeDtypeStruct((2, *block), jnp.bfloat16),
            jax.ShapeDtypeStruct(block, jnp.float32),
            jax.ShapeDtypeStruct(block, jnp.float32),
        ],
        compiler_params=PARAMS,
        name="partial_products",
    )(info, left, partner, *pieces)


def combine_kernel(chunk, position, core, mine, a, b, *refs):
    rdm, others, turned, own, other, block, sems = refs[-7:]
    rows, cols = own.shape
    f32 = jnp.float32
    total = (mine[...] + a[0].astype(f32)) + b[...].astype(f32)
    own[...] = total[0].astype(jnp.bfloat16)
    other[...] = total[1].astype(jnp.bfloat16)
    at = pl.multiple_of(core[0] * rows + chunk * cols, 128)
    copies = [
        pltpu.make_async_copy(own, rdm.at[:, pl.ds(at, cols)], sems.at[0]),
        pltpu.make_async_copy(other, others.at[:, pl.ds(chunk * cols, cols)], sems.at[1]),
        pltpu.make_async_copy(block, turned.at[position], sems.at[2]),
    ]
    for copy in copies[:2]:
        copy.start()
    width = block.shape[0]
    by_row = total.reshape(2 * rows // width, width, cols)
    block[...] = jnp.swapaxes(by_row, 0, 1).astype(jnp.bfloat16)
    copies[2].start()
    for copy in copies:
        copy.wait()


def combine(chunk, group, core, mine, near, far, width, pair_cols, held):
    _, rows, cols = mine.shape
    bf16 = jnp.bfloat16
    block = (width, 2 * rows // width, cols)
    return pl.pallas_call(
        functools.partial(combine_kernel, chunk, group.index(chunk)),
        in_specs=[SMEM] + [VMEM] * 3 + [HBM] * len(held),
        out_specs=[HBM] * 3,
        out_shape=[
            jax.ShapeDtypeStruct((rows, pair_cols), bf16),
            jax.ShapeDtypeStruct((rows, pair_cols // 2), bf16),
            jax.ShapeDtypeStruct((len(group), *block), bf16),
        ],
        scratch_shapes=[pltpu.VMEM((rows, cols), bf16)] * 2
        + [pltpu.VMEM(block, bf16), pltpu.SemaphoreType.DMA((3,))],
        input_output_aliases={4 + i: i for i in range(len(held))},
        compiler_params=PARAMS,
        name="combine",
    )(core, mine, near, far, *held)


def place_kernel(core, other, held, rdm, sem):
    rows = other.shape[1]
    at = pl.multiple_of((1 - core[0]) * rows, 128)
    copy = pltpu.make_async_copy(other, rdm.at[:, pl.ds(at, rows)], sem)
    copy.start()
    copy.wait()


def place(core, other, rdm):
    return pl.pallas_call(
        place_kernel,
        in_specs=[SMEM, VMEM, HBM],
        out_specs=HBM,
        out_shape=jax.ShapeDtypeStruct(rdm.shape, rdm.dtype),
        scratch_shapes=[pltpu.SemaphoreType.DMA],
        input_output_aliases={2: 0},
        compiler_params=PARAMS,
        name="place",
    )(core, other, rdm)


def fock_kernel(first, base, slab, diagonal, *refs):
    *pieces, fock, traced, part, rdm, sems = refs
    width, orbitals, total = part.shape
    chunks, _, _, cols = pieces[0].shape
    copies = [pltpu.make_async_copy(slab.at[:, :, pl.ds(first * cols, total)], part, sems.at[4])]
    for r in range(4):
        piece = pieces[r] if len(pieces) == 4 else pieces[min(r, 2)]
        if len(pieces) == 3 and r >= 2:
            piece = piece.at[pl.ds((r - 2) * chunks, chunks)]
        copies.append(pltpu.make_async_copy(piece, rdm.at[base[0] ^ r], sems.at[r]))
    for copy in copies:
        copy.start()
    for copy in copies:
        copy.wait()
    acc = jnp.zeros((orbitals, width), jnp.float32)
    for u in range(width):
        trace = None
        for n in range(chunks):
            at = slice(n * cols, (n + 1) * cols)
            lhs = jnp.concatenate([part[u, :, at], diagonal[:, at]], axis=0)
            rhs = jnp.concatenate([rdm[c, n, u] for c in range(4)], axis=0)
            out = lax.dot_general(lhs, rhs, NT, preferred_element_type=jnp.float32)
            acc += out[:orbitals]
            trace = out[orbitals] if trace is None else trace + out[orbitals]
        traced[u, :] = trace
    fock[...] = acc


def fock_terms(first, base, slab, diagonal, *pieces):
    width, orbitals, _ = slab.shape
    chunks, _, _, cols = pieces[0].shape
    return pl.pallas_call(
        functools.partial(fock_kernel, first),
        in_specs=[SMEM, HBM, VMEM] + [HBM] * len(pieces),
        out_specs=[VMEM] * 2,
        out_shape=[
            jax.ShapeDtypeStruct((orbitals, width), jnp.float32),
            jax.ShapeDtypeStruct((width, width), jnp.float32),
        ],
        scratch_shapes=[
            pltpu.VMEM((width, orbitals, chunks * cols), jnp.bfloat16),
            pltpu.VMEM((4, *pieces[0].shape), jnp.bfloat16),
            pltpu.SemaphoreType.DMA((5,)),
        ],
        compiler_params=PARAMS,
        name="fock_terms",
    )(base, slab, diagonal, *pieces)


def turn_kernel(core, a, b, o):
    size = a.shape[0]
    o[:, :size] = jnp.swapaxes(a[...].astype(jnp.float32), 0, 1).astype(jnp.bfloat16)
    o[:, size:] = jnp.swapaxes(b[...].astype(jnp.float32), 0, 1).astype(jnp.bfloat16)


def turn(core, slab, received, cols):
    orbitals, width, total = received.shape
    steps = total // cols
    return pl.pallas_call(
        turn_kernel,
        grid_spec=pltpu.PrefetchScalarGridSpec(
            num_scalar_prefetch=1,
            grid=(steps,),
            in_specs=[
                pl.BlockSpec((orbitals, width, cols), lambda i, core: (0, 0, core[0] * steps + i)),
                pl.BlockSpec((orbitals, width, cols), lambda i, core: (0, 0, i)),
            ],
            out_specs=pl.BlockSpec((width, 2 * orbitals, cols), lambda i, core: (0, 0, i)),
        ),
        out_shape=jax.ShapeDtypeStruct((width, 2 * orbitals, total), jnp.bfloat16),
        compiler_params=PARAMS,
        name="turn",
    )(core, slab, received)


def after(value, *done):
    done = jax.tree.leaves(done)
    return lax.optimization_barrier((value, *done))[0]


def shards(secs, gens, amps_left, amps_right, block_sizes, slab, fcore):
    sectors, rows, states = amps_left.shape
    general, width, pair_cols = slab.shape
    cols = rows // CHUNKS
    half = cols // 2
    z = lax.axis_index("sec")
    g = lax.axis_index("gen")
    chip, core = g // 2, g % 2

    def across(value, flip):
        return lax.ppermute(value, "gen", [(i, i ^ flip) for i in range(gens)])

    def along(value, flip):
        return lax.ppermute(value, "sec", [(i, i ^ flip) for i in range(secs)])

    def number(value):
        return value.reshape(1).astype(jnp.int32)

    def bra(chunk, source):
        return source[:, chunk * cols : (chunk + 1) * cols]

    sent = bra(0, amps_right)
    pieces = {}
    if ORDER[0] == "W0":
        xs, ys = across(sent, 2), across(sent, 4)
    else:
        pieces[0] = [across(sent, 2 * r) for r in (1, 2, 3)]
    partner_left = across(amps_left, 1)
    later = after(amps_right, sent)
    waiting = [None] + [bra(chunk, later) for chunk in range(1, CHUNKS)]

    given = lax.dynamic_slice(after(slab, sent), (0, 0, (1 - core) * rows), (general, width, rows))
    received, *waiting[1:] = lax.optimization_barrier((across(given, 1), *waiting[1:]))
    integrals = turn(number(core), slab, received, cols)

    column_ids = z * pair_cols + core * rows + jnp.arange(rows, dtype=jnp.int32)
    diagonal = jnp.broadcast_to(
        (column_ids // width == column_ids % width).astype(jnp.bfloat16)[None], (16, rows)
    )

    def products(chunk, *parts):
        mine = slice(chunk * cols, (chunk + 1) * cols)
        every = slice(None)
        cuts = [(0, (every, mine), 0, 0)] + [(n, (every,), 0, n) for n in range(1, 4)]
        if len(parts) == 4:
            cuts.append((4, (every,), half, 3))
        info = jnp.concatenate([number(chip ^ z), block_sizes])
        return partial_products(info, amps_left, partner_left, cols, cuts, amps_right, *parts)

    sums, terms, gathered = [None] * CHUNKS, [], {}

    def contract(group):
        at = slice(group[0] * cols, (group[-1] + 1) * cols)
        marks = after(diagonal[:, at], state["last"])
        terms.append(fock_terms(group[0], number(chip), integrals, marks, *gathered[group]))
        state["last"] = terms[-1][0]

    if 0 in pieces:
        state = {"last": (), "held": ()}
        sent = after(waiting[1], *pieces[0], integrals)
        state["xs"], state["ys"] = across(sent, 2), across(sent, 4)
    else:
        state = {"last": integrals, "held": (), "xs": xs, "ys": ys}

    def do_forward(chunk):
        last = state["last"]
        xs, ys = after(state["xs"], last), after(state["ys"], last)
        lower, upper = xs[:, :half], ys[:, half:]
        pieces[chunk] = (xs, ys, across(lower, 4), across(upper, 2))
        state["last"] = (lower, upper)
        if chunk + 1 < CHUNKS:
            sent = after(waiting[chunk + 1], xs, ys)
            state["xs"], state["ys"] = across(sent, 2), across(sent, 4)

    def do_products(chunk):
        near, own, far = products(chunk, *(after(p, state["last"]) for p in pieces[chunk]))
        sums[chunk] = [own, along(near, 1), far]
        state["last"] = own

    def do_pass(chunk):
        own, near, far = sums[chunk]
        far = after(far, state["last"])
        passed = (far + near[1].astype(jnp.float32)).astype(jnp.bfloat16)
        sums[chunk] = [own, near, along(passed, 2)]
        state["last"] = passed

    def do_finish(chunk):
        own, near, far = sums[chunk]
        group = [g for g in GROUPS if chunk in g][0]
        held = state["held"] if chunk > group[0] else state["held"][:2]
        state["held"] = combine(
            chunk, group, number(core), after(own, state["last"]), near, far, width, pair_cols, held
        )
        turned = state["held"][2]
        if chunk == group[-1]:
            if True:
                gathered[group] = (turned, *[across(turned, 2 * r) for r in (1, 2, 3)])
            else:
                gathered[group] = (turned, across(turned, 2))
        state["last"] = state["held"][1]

    def do_second(chunk):
        group = [g for g in GROUPS if chunk in g][0]
        both = jnp.concatenate([after(p, state["last"]) for p in gathered[group]], axis=0)
        gathered[group] += (across(both, 4),)
        state["last"] = both

    def do_wait(chunk):
        state["last"] = (state["last"], *pieces[chunk][2:])

    steps = {
        "W": do_forward,
        "A": do_wait,
        "M": do_products,
        "P": do_pass,
        "C": do_finish,
        "H": do_second,
        "F": lambda chunk: contract([g for g in GROUPS if chunk in g][0]),
    }
    for step in ORDER:
        if step == "R":
            rdm = place(number(core), across(state["held"][1], 1), state["held"][0])
            state["last"] = rdm
        else:
            steps[step[0]](int(step[1]))

    two_body = sum(t[0] for t in terms)
    traced = sum(t[1] for t in terms)

    def ordered(value):
        split = value.reshape(value.shape[0], 4, 2, -1)
        return jnp.where(core == 0, split, split[:, :, ::-1]).reshape(value.shape)

    one = ordered(traced).T / width
    both = jnp.concatenate([fcore, across(fcore, 1)], axis=0).astype(jnp.float32)
    mine = ordered(two_body) + jnp.dot(both, one, precision=lax.Precision.HIGHEST)
    theirs = across(mine, 1)
    fock = mine[:general] + theirs[general:]
    partner = mine[general:] + theirs[:general]

    first = jnp.where(core == 0, fock, partner)
    second = jnp.where(core == 0, partner, fock)
    active = jnp.concatenate([first, second], axis=0)
    flipped = lax.dynamic_slice_in_dim(active.T, core * general, general, axis=0)
    part = 2.0 * (fock - jnp.where(g < 2, flipped, 0.0))
    for flip in (1, 2):
        part = part + along(part, flip)
    return rdm, part


def general_shards(secs, gens, amps_left, amps_right, block_sizes, slab, fcore):
    sectors, rows, states = amps_left.shape
    general, width, pair_cols = slab.shape
    chips = gens // 2
    per_sec = chips // secs
    bits = chips.bit_length() - 1
    chunks = 1
    half = rows // chunks // 2
    z = lax.axis_index("sec")
    g = lax.axis_index("gen")
    chip, core = g // 2, g % 2

    def across(value, flip):
        return lax.ppermute(value, "gen", [(i, i ^ flip) for i in range(gens)])

    def along(value, flip):
        return lax.ppermute(value, "sec", [(i, i ^ flip) for i in range(secs)])

    def gather(value, order):
        held = value[None]
        for bit in order:
            held = jnp.concatenate([held, across(held, 2 << bit)], axis=0)
        return held

    def place(relative, order):
        return sum(((relative >> bit) & 1) << at for at, bit in enumerate(order))

    orders = (tuple(range(bits)), tuple(reversed(range(bits))))
    live = (jnp.arange(states, dtype=jnp.int32)[None, :] < block_sizes[:, None]).astype(jnp.bfloat16)

    left = jnp.concatenate([amps_left, across(amps_left, 1)], axis=1) * live[:, None, :]

    by_core = slab.reshape(general, width, per_sec, 2, rows)
    kept = lax.dynamic_index_in_dim(by_core, core, 3, keepdims=False)
    given = lax.dynamic_index_in_dim(by_core, 1 - core, 3, keepdims=False)
    integrals = jnp.concatenate([kept, across(given, 1)], axis=0)

    column_ids = (
        z * pair_cols
        + jnp.arange(per_sec, dtype=jnp.int32)[:, None] * (2 * rows)
        + core * rows
        + jnp.arange(rows, dtype=jnp.int32)[None, :]
    )
    diagonal = (column_ids // width == column_ids % width).astype(jnp.bfloat16)

    pieces = []
    two_body = jnp.zeros((2 * general, width), jnp.float32)
    traced = jnp.zeros((width, width), jnp.float32)
    for chunk in range(chunks):
        start = chunk * 2 * half
        blocks = [
            gather(amps_right[:, start + i * half : start + (i + 1) * half], orders[i])
            for i in range(2)
        ]

        def partial_for(dest):
            wanted = chip ^ (dest * per_sec + jnp.arange(per_sec, dtype=jnp.int32))
            found = [
                jnp.take(blocks[i], place(wanted, orders[i]), axis=0) for i in range(2)
            ]
            right = jnp.concatenate(found, axis=2)
            return jnp.einsum(
                "srm,csqm->rcq", left, right, preferred_element_type=jnp.float32
            )

        arrived = [
            along(partial_for(z ^ flip).astype(jnp.bfloat16), flip) for flip in range(1, secs)
        ]
        total = partial_for(z)
        for value in arrived:
            total = total + value.astype(jnp.float32)
        piece = total.astype(jnp.bfloat16)
        pieces.append(piece)

        columns = per_sec * 2 * half
        by_row = piece.reshape(2, rows // width, width, columns)
        halves = [gather(by_row[i], orders[i]) for i in range(2)]
        table = jnp.arange(chips, dtype=jnp.int32)
        halves[1] = halves[1][jnp.array([sum(((p >> b) & 1) << a for a, b in enumerate(orders[1])) for p in range(chips)])]
        every = jnp.stack(halves, axis=1).reshape(width, width, columns)
        part = integrals[:, :, :, start : start + 2 * half].reshape(2 * general, width, columns)
        two_body = two_body + jnp.einsum(
            "puq,tuq->pt", part, every, preferred_element_type=jnp.float32
        )
        traced = traced + jnp.einsum(
            "tuq,q->tu",
            every,
            diagonal[:, start : start + 2 * half].reshape(columns),
            preferred_element_type=jnp.float32,
        )

    def ordered(value, axis):
        shape = value.shape
        split = value.reshape(shape[:axis] + (gens, shape[axis] // gens) + shape[axis + 1 :])
        return jnp.take(split, g ^ jnp.arange(gens), axis=axis).reshape(shape)

    two_body = ordered(two_body, 1)
    one = ordered(traced, 0) / width
    both = jnp.concatenate([fcore, across(fcore, 1)], axis=0).astype(jnp.float32)
    mine = two_body + jnp.dot(both, one, precision=lax.Precision.HIGHEST)
    theirs = across(mine, 1)
    fock = mine[:general] + theirs[general:]
    partner = mine[general:] + theirs[:general]

    first = jnp.where(core == 0, fock, partner)
    second = jnp.where(core == 0, partner, fock)
    active = jnp.concatenate([first, second], axis=0)
    flipped = lax.dynamic_slice_in_dim(active.T, core * general, general, axis=0)
    part = 2.0 * (fock - jnp.where(g < 2, flipped, 0.0))
    parts = [part] + [along(part, flip) for flip in range(1, secs)]
    while len(parts) > 1:
        parts = [a + b for a, b in zip(parts[::2], parts[1::2])]
    grad = parts[0]

    own = jnp.concatenate([p[:rows] for p in pieces], axis=2)
    other = across(jnp.concatenate([p[rows:] for p in pieces], axis=2), 1)
    lower = jnp.where(core == 0, own, other)
    upper = jnp.where(core == 0, other, own)
    rdm = jnp.stack([lower, upper], axis=2).reshape(rows, pair_cols)
    return rdm, grad


def solution(mesh):
    secs, gens = mesh.shape["sec"], mesh.shape["gen"]
    placed = (
        P("sec", "gen", None),
        P("sec", "gen", None),
        P("sec"),
        P("gen", None, "sec"),
        P("gen", None),
    )
    def step(*args):
        rows, general, width = args[0].shape[1], args[3].shape[0], args[3].shape[1]
        fits = secs == 4 and gens == 8 and 2 * general == width and rows == 128 * CHUNKS
        return (shards if fits else general_shards)(secs, gens, *args)

    return jax.shard_map(
        step,
        mesh=mesh,
        in_specs=placed,
        out_specs=(P("gen", "sec"), P("gen", None)),
        check_vma=False,
    )
```

```python
import functools

import jax
import jax.numpy as jnp
from jax import lax
from jax.experimental import pallas as pl
from jax.experimental.pallas import tpu as pltpu
from jax.sharding import PartitionSpec as P

CHUNKS = 4
GROUPS = ((0,), (1,), (2,), (3,))
ORDER = (
    "W0", "M0", "W1", "A1", "P0", "M1", "W2", "A2", "P1", "M2", "C0", "W3", "A3", "P2", "C1", "M3", "F0", "C2", "F1", "P3", "F2", "C3", "R", "F3",
)
LIMIT = 50 * 2**20
NT = (((1,), (1,)), ((), ()))
HBM = pl.BlockSpec(memory_space=pltpu.HBM)
VMEM = pl.BlockSpec(memory_space=pltpu.VMEM)
SMEM = pl.BlockSpec(memory_space=pltpu.SMEM)
PARAMS = pltpu.CompilerParams(vmem_limit_bytes=LIMIT)


def partial_kernel(cuts, info, left, partner, *refs):
    *pieces, near, own, far, bra, ket, bra_sem, ket_sem = refs
    sectors, rows, states = left.shape
    cols = own.shape[2]
    copies = []
    for n, (ref, index, start, r) in enumerate(cuts):
        piece = pieces[ref].at[index]
        at = pl.multiple_of((info[0] ^ r) * cols + start, 16)
        copies.append(pltpu.make_async_copy(piece, bra.at[:, pl.ds(at, piece.shape[1])], bra_sem.at[n]))
    kets = [
        pltpu.make_async_copy(ref, ket.at[c], ket_sem.at[c]) for c, ref in enumerate((left, partner))
    ]
    for copy in copies + kets:
        copy.start()
    for copy in copies:
        copy.wait()
    ids = lax.broadcasted_iota(jnp.int32, (rows, states), 1)
    for c in range(2):
        kets[c].wait()
        out = None
        for s in range(sectors):
            live = jnp.where(ids < info[1 + s], ket[c, s].astype(jnp.float32), 0.0)
            term = lax.dot_general(
                live.astype(jnp.bfloat16), bra[s], NT, preferred_element_type=jnp.float32
            )
            out = term if out is None else out + term
        blocks = [out[:, k * cols : (k + 1) * cols] for k in range(4)]
        own[c] = blocks[0]
        near[0, c] = blocks[1].astype(jnp.bfloat16)
        near[1, c] = blocks[3].astype(jnp.bfloat16)
        far[c] = blocks[2].astype(far.dtype)


def partial_products(info, left, partner, cols, cuts, *pieces):
    sectors, rows, states = left.shape

    block = (2, rows, cols)
    return pl.pallas_call(
        functools.partial(partial_kernel, cuts),
        in_specs=[SMEM] + [HBM] * (2 + len(pieces)),
        out_specs=[VMEM] * 3,
        scratch_shapes=[
            pltpu.VMEM((sectors, 4 * cols, states), jnp.bfloat16),
            pltpu.VMEM((2, sectors, rows, states), jnp.bfloat16),
            pltpu.SemaphoreType.DMA((len(cuts),)),
            pltpu.SemaphoreType.DMA((2,)),
        ],
        out_shape=[
            jax.ShapeDtypeStruct((2, *block), jnp.bfloat16),
            jax.ShapeDtypeStruct(block, jnp.float32),
            jax.ShapeDtypeStruct(block, jnp.float32),
        ],
        compiler_params=PARAMS,
        cost_estimate=pl.CostEstimate(flops=2147483648, bytes_accessed=1, transcendentals=0),
        name="partial_products",
    )(info, left, partner, *pieces)


def combine_kernel(chunk, position, core, mine, a, b, *refs):
    rdm, others, turned, own, other, block, sems = refs[-7:]
    rows, cols = own.shape
    f32 = jnp.float32
    total = (mine[...] + a[0].astype(f32)) + b[...].astype(f32)
    own[...] = total[0].astype(jnp.bfloat16)
    other[...] = total[1].astype(jnp.bfloat16)
    at = pl.multiple_of(core[0] * rows + chunk * cols, 128)
    copies = [
        pltpu.make_async_copy(own, rdm.at[:, pl.ds(at, cols)], sems.at[0]),
        pltpu.make_async_copy(other, others.at[:, pl.ds(chunk * cols, cols)], sems.at[1]),
        pltpu.make_async_copy(block, turned.at[position], sems.at[2]),
    ]
    for copy in copies[:2]:
        copy.start()
    width = block.shape[0]
    by_row = total.reshape(2 * rows // width, width, cols)
    block[...] = jnp.swapaxes(by_row, 0, 1).astype(jnp.bfloat16)
    copies[2].start()
    for copy in copies:
        copy.wait()


def combine(chunk, group, core, mine, near, far, width, pair_cols, held):
    _, rows, cols = mine.shape
    bf16 = jnp.bfloat16
    block = (width, 2 * rows // width, cols)
    return pl.pallas_call(
        functools.partial(combine_kernel, chunk, group.index(chunk)),
        in_specs=[SMEM] + [VMEM] * 3 + [HBM] * len(held),
        out_specs=[HBM] * 3,
        out_shape=[
            jax.ShapeDtypeStruct((rows, pair_cols), bf16),
            jax.ShapeDtypeStruct((rows, pair_cols // 2), bf16),
            jax.ShapeDtypeStruct((len(group), *block), bf16),
        ],
        scratch_shapes=[pltpu.VMEM((rows, cols), bf16)] * 2
        + [pltpu.VMEM(block, bf16), pltpu.SemaphoreType.DMA((3,))],
        input_output_aliases={4 + i: i for i in range(len(held))},
        compiler_params=PARAMS,
        cost_estimate=pl.CostEstimate(flops=1048576, bytes_accessed=1, transcendentals=0),
        name="combine",
    )(core, mine, near, far, *held)


def place_kernel(core, other, held, rdm, sem):
    rows = other.shape[1]
    at = pl.multiple_of((1 - core[0]) * rows, 128)
    copy = pltpu.make_async_copy(other, rdm.at[:, pl.ds(at, rows)], sem)
    copy.start()
    copy.wait()


def place(core, other, rdm):
    return pl.pallas_call(
        place_kernel,
        in_specs=[SMEM, VMEM, HBM],
        out_specs=HBM,
        out_shape=jax.ShapeDtypeStruct(rdm.shape, rdm.dtype),
        scratch_shapes=[pltpu.SemaphoreType.DMA],
        input_output_aliases={2: 0},
        compiler_params=PARAMS,
        name="place",
    )(core, other, rdm)


def fock_kernel(first, base, slab, diagonal, *refs):
    *pieces, fock, traced, part, rdm, sems = refs
    width, orbitals, total = part.shape
    chunks, _, _, cols = pieces[0].shape
    copies = [pltpu.make_async_copy(slab.at[:, :, pl.ds(first * cols, total)], part, sems.at[4])]
    for r in range(4):
        piece = pieces[r] if len(pieces) == 4 else pieces[min(r, 2)]
        if len(pieces) == 3 and r >= 2:
            piece = piece.at[pl.ds((r - 2) * chunks, chunks)]
        copies.append(pltpu.make_async_copy(piece, rdm.at[base[0] ^ r], sems.at[r]))
    for copy in copies:
        copy.start()
    for copy in copies:
        copy.wait()
    acc = jnp.zeros((orbitals, width), jnp.float32)
    for u in range(width):
        trace = None
        for n in range(chunks):
            at = slice(n * cols, (n + 1) * cols)
            lhs = jnp.concatenate([part[u, :, at], diagonal[:, at]], axis=0)
            rhs = jnp.concatenate([rdm[c, n, u] for c in range(4)], axis=0)
            out = lax.dot_general(lhs, rhs, NT, preferred_element_type=jnp.float32)
            acc += out[:orbitals]
            trace = out[orbitals] if trace is None else trace + out[orbitals]
        traced[u, :] = trace
    fock[...] = acc


def fock_terms(first, base, slab, diagonal, *pieces):
    width, orbitals, _ = slab.shape
    chunks, _, _, cols = pieces[0].shape
    return pl.pallas_call(
        functools.partial(fock_kernel, first),
        in_specs=[SMEM, HBM, VMEM] + [HBM] * len(pieces),
        out_specs=[VMEM] * 2,
        out_shape=[
            jax.ShapeDtypeStruct((orbitals, width), jnp.float32),
            jax.ShapeDtypeStruct((width, width), jnp.float32),
        ],
        scratch_shapes=[
            pltpu.VMEM((width, orbitals, chunks * cols), jnp.bfloat16),
            pltpu.VMEM((4, *pieces[0].shape), jnp.bfloat16),
            pltpu.SemaphoreType.DMA((5,)),
        ],
        compiler_params=PARAMS,
        cost_estimate=pl.CostEstimate(flops=83886080, bytes_accessed=1, transcendentals=0),
        name="fock_terms",
    )(base, slab, diagonal, *pieces)


def turn_kernel(core, a, b, o):
    size = a.shape[0]
    o[:, :size] = jnp.swapaxes(a[...].astype(jnp.float32), 0, 1).astype(jnp.bfloat16)
    o[:, size:] = jnp.swapaxes(b[...].astype(jnp.float32), 0, 1).astype(jnp.bfloat16)


def turn(core, slab, received, cols):
    orbitals, width, total = received.shape
    steps = total // cols
    return pl.pallas_call(
        turn_kernel,
        grid_spec=pltpu.PrefetchScalarGridSpec(
            num_scalar_prefetch=1,
            grid=(steps,),
            in_specs=[
                pl.BlockSpec((orbitals, width, cols), lambda i, core: (0, 0, core[0] * steps + i)),
                pl.BlockSpec((orbitals, width, cols), lambda i, core: (0, 0, i)),
            ],
            out_specs=pl.BlockSpec((width, 2 * orbitals, cols), lambda i, core: (0, 0, i)),
        ),
        out_shape=jax.ShapeDtypeStruct((width, 2 * orbitals, total), jnp.bfloat16),
        compiler_params=PARAMS,
        cost_estimate=pl.CostEstimate(flops=1048576, bytes_accessed=1, transcendentals=0),
        name="turn",
    )(core, slab, received)


def after(value, *done):
    done = jax.tree.leaves(done)
    return lax.optimization_barrier((value, *done))[0]


def shards(secs, gens, amps_left, amps_right, block_sizes, slab, fcore):
    sectors, rows, states = amps_left.shape
    general, width, pair_cols = slab.shape
    cols = rows // CHUNKS
    half = cols // 2
    z = lax.axis_index("sec")
    g = lax.axis_index("gen")
    chip, core = g // 2, g % 2

    def across(value, flip):
        return lax.ppermute(value, "gen", [(i, i ^ flip) for i in range(gens)])

    def along(value, flip):
        return lax.ppermute(value, "sec", [(i, i ^ flip) for i in range(secs)])

    def number(value):
        return value.reshape(1).astype(jnp.int32)

    def bra(chunk, source):
        return source[:, chunk * cols : (chunk + 1) * cols]

    sent = bra(0, amps_right)
    pieces = {}
    if ORDER[0] == "W0":
        xs, ys = across(sent, 2), across(sent, 4)
    else:
        pieces[0] = [across(sent, 2 * r) for r in (1, 2, 3)]
    partner_left = across(amps_left, 1)
    later = after(amps_right, sent)
    waiting = [None] + [bra(chunk, later) for chunk in range(1, CHUNKS)]

    given = lax.dynamic_slice(after(slab, sent), (0, 0, (1 - core) * rows), (general, width, rows))
    received, *waiting[1:] = lax.optimization_barrier((across(given, 1), *waiting[1:]))
    integrals = turn(number(core), slab, received, cols)

    column_ids = z * pair_cols + core * rows + jnp.arange(rows, dtype=jnp.int32)
    diagonal = jnp.broadcast_to(
        (column_ids // width == column_ids % width).astype(jnp.bfloat16)[None], (16, rows)
    )

    def products(chunk, *parts):
        mine = slice(chunk * cols, (chunk + 1) * cols)
        every = slice(None)
        cuts = [(0, (every, mine), 0, 0)] + [(n, (every,), 0, n) for n in range(1, 4)]
        if len(parts) == 4:
            cuts.append((4, (every,), half, 3))
        info = jnp.concatenate([number(chip ^ z), block_sizes])
        return partial_products(info, amps_left, partner_left, cols, cuts, amps_right, *parts)

    sums, terms, gathered = [None] * CHUNKS, [], {}

    def contract(group):
        at = slice(group[0] * cols, (group[-1] + 1) * cols)
        marks = after(diagonal[:, at], state["last"])
        terms.append(fock_terms(group[0], number(chip), integrals, marks, *gathered[group]))
        state["last"] = terms[-1][0]

    if 0 in pieces:
        state = {"last": (), "held": ()}
        sent = after(waiting[1], *pieces[0], integrals)
        state["xs"], state["ys"] = across(sent, 2), across(sent, 4)
    else:
        state = {"last": integrals, "held": (), "xs": xs, "ys": ys}

    def do_forward(chunk):
        last = state["last"]
        xs, ys = after(state["xs"], last), after(state["ys"], last)
        lower, upper = xs[:, :half], ys[:, half:]
        pieces[chunk] = (xs, ys, across(lower, 4), across(upper, 2))
        state["last"] = (lower, upper)
        if chunk + 1 < CHUNKS:
            sent = after(waiting[chunk + 1], xs, ys)
            state["xs"], state["ys"] = across(sent, 2), across(sent, 4)

    def do_products(chunk):
        near, own, far = products(chunk, *(after(p, state["last"]) for p in pieces[chunk]))
        sums[chunk] = [own, along(near, 1), far]
        state["last"] = own

    def do_pass(chunk):
        own, near, far = sums[chunk]
        far = after(far, state["last"])
        passed = (far + near[1].astype(jnp.float32)).astype(jnp.bfloat16)
        sums[chunk] = [own, near, along(passed, 2)]
        state["last"] = passed

    def do_finish(chunk):
        own, near, far = sums[chunk]
        group = [g for g in GROUPS if chunk in g][0]
        held = state["held"] if chunk > group[0] else state["held"][:2]
        state["held"] = combine(
            chunk, group, number(core), after(own, state["last"]), near, far, width, pair_cols, held
        )
        turned = state["held"][2]
        if chunk == group[-1]:
            if True:
                gathered[group] = (turned, *[across(turned, 2 * r) for r in (1, 2, 3)])
            else:
                gathered[group] = (turned, across(turned, 2))
        state["last"] = state["held"][1]

    def do_second(chunk):
        group = [g for g in GROUPS if chunk in g][0]
        both = jnp.concatenate([after(p, state["last"]) for p in gathered[group]], axis=0)
        gathered[group] += (across(both, 4),)
        state["last"] = both

    def do_wait(chunk):
        state["last"] = (state["last"], *pieces[chunk][2:])

    steps = {
        "W": do_forward,
        "A": do_wait,
        "M": do_products,
        "P": do_pass,
        "C": do_finish,
        "H": do_second,
        "F": lambda chunk: contract([g for g in GROUPS if chunk in g][0]),
    }
    for step in ORDER:
        if step == "R":
            rdm = place(number(core), across(state["held"][1], 1), state["held"][0])
            state["last"] = rdm
        else:
            steps[step[0]](int(step[1]))

    two_body = sum(t[0] for t in terms)
    traced = sum(t[1] for t in terms)

    def ordered(value):
        split = value.reshape(value.shape[0], 4, 2, -1)
        return jnp.where(core == 0, split, split[:, :, ::-1]).reshape(value.shape)

    one = ordered(traced).T / width
    both = jnp.concatenate([fcore, across(fcore, 1)], axis=0).astype(jnp.float32)
    mine = ordered(two_body) + jnp.dot(both, one, precision=lax.Precision.HIGHEST)
    theirs = across(mine, 1)
    fock = mine[:general] + theirs[general:]
    partner = mine[general:] + theirs[:general]

    first = jnp.where(core == 0, fock, partner)
    second = jnp.where(core == 0, partner, fock)
    active = jnp.concatenate([first, second], axis=0)
    flipped = lax.dynamic_slice_in_dim(active.T, core * general, general, axis=0)
    part = 2.0 * (fock - jnp.where(g < 2, flipped, 0.0))
    for flip in (1, 2):
        part = part + along(part, flip)
    return rdm, part


def general_shards(secs, gens, amps_left, amps_right, block_sizes, slab, fcore):
    sectors, rows, states = amps_left.shape
    general, width, pair_cols = slab.shape
    chips = gens // 2
    per_sec = chips // secs
    bits = chips.bit_length() - 1
    chunks = 1
    half = rows // chunks // 2
    z = lax.axis_index("sec")
    g = lax.axis_index("gen")
    chip, core = g // 2, g % 2

    def across(value, flip):
        return lax.ppermute(value, "gen", [(i, i ^ flip) for i in range(gens)])

    def along(value, flip):
        return lax.ppermute(value, "sec", [(i, i ^ flip) for i in range(secs)])

    def gather(value, order):
        held = value[None]
        for bit in order:
            held = jnp.concatenate([held, across(held, 2 << bit)], axis=0)
        return held

    def place(relative, order):
        return sum(((relative >> bit) & 1) << at for at, bit in enumerate(order))

    orders = (tuple(range(bits)), tuple(reversed(range(bits))))
    live = (jnp.arange(states, dtype=jnp.int32)[None, :] < block_sizes[:, None]).astype(jnp.bfloat16)

    left = jnp.concatenate([amps_left, across(amps_left, 1)], axis=1) * live[:, None, :]

    by_core = slab.reshape(general, width, per_sec, 2, rows)
    kept = lax.dynamic_index_in_dim(by_core, core, 3, keepdims=False)
    given = lax.dynamic_index_in_dim(by_core, 1 - core, 3, keepdims=False)
    integrals = jnp.concatenate([kept, across(given, 1)], axis=0)

    column_ids = (
        z * pair_cols
        + jnp.arange(per_sec, dtype=jnp.int32)[:, None] * (2 * rows)
        + core * rows
        + jnp.arange(rows, dtype=jnp.int32)[None, :]
    )
    diagonal = (column_ids // width == column_ids % width).astype(jnp.bfloat16)

    pieces = []
    two_body = jnp.zeros((2 * general, width), jnp.float32)
    traced = jnp.zeros((width, width), jnp.float32)
    for chunk in range(chunks):
        start = chunk * 2 * half
        blocks = [
            gather(amps_right[:, start + i * half : start + (i + 1) * half], orders[i])
            for i in range(2)
        ]

        def partial_for(dest):
            wanted = chip ^ (dest * per_sec + jnp.arange(per_sec, dtype=jnp.int32))
            found = [
                jnp.take(blocks[i], place(wanted, orders[i]), axis=0) for i in range(2)
            ]
            right = jnp.concatenate(found, axis=2)
            return jnp.einsum(
                "srm,csqm->rcq", left, right, preferred_element_type=jnp.float32
            )

        arrived = [
            along(partial_for(z ^ flip).astype(jnp.bfloat16), flip) for flip in range(1, secs)
        ]
        total = partial_for(z)
        for value in arrived:
            total = total + value.astype(jnp.float32)
        piece = total.astype(jnp.bfloat16)
        pieces.append(piece)

        columns = per_sec * 2 * half
        by_row = piece.reshape(2, rows // width, width, columns)
        halves = [gather(by_row[i], orders[i]) for i in range(2)]
        table = jnp.arange(chips, dtype=jnp.int32)
        halves[1] = halves[1][jnp.array([sum(((p >> b) & 1) << a for a, b in enumerate(orders[1])) for p in range(chips)])]
        every = jnp.stack(halves, axis=1).reshape(width, width, columns)
        part = integrals[:, :, :, start : start + 2 * half].reshape(2 * general, width, columns)
        two_body = two_body + jnp.einsum(
            "puq,tuq->pt", part, every, preferred_element_type=jnp.float32
        )
        traced = traced + jnp.einsum(
            "tuq,q->tu",
            every,
            diagonal[:, start : start + 2 * half].reshape(columns),
            preferred_element_type=jnp.float32,
        )

    def ordered(value, axis):
        shape = value.shape
        split = value.reshape(shape[:axis] + (gens, shape[axis] // gens) + shape[axis + 1 :])
        return jnp.take(split, g ^ jnp.arange(gens), axis=axis).reshape(shape)

    two_body = ordered(two_body, 1)
    one = ordered(traced, 0) / width
    both = jnp.concatenate([fcore, across(fcore, 1)], axis=0).astype(jnp.float32)
    mine = two_body + jnp.dot(both, one, precision=lax.Precision.HIGHEST)
    theirs = across(mine, 1)
    fock = mine[:general] + theirs[general:]
    partner = mine[general:] + theirs[:general]

    first = jnp.where(core == 0, fock, partner)
    second = jnp.where(core == 0, partner, fock)
    active = jnp.concatenate([first, second], axis=0)
    flipped = lax.dynamic_slice_in_dim(active.T, core * general, general, axis=0)
    part = 2.0 * (fock - jnp.where(g < 2, flipped, 0.0))
    parts = [part] + [along(part, flip) for flip in range(1, secs)]
    while len(parts) > 1:
        parts = [a + b for a, b in zip(parts[::2], parts[1::2])]
    grad = parts[0]

    own = jnp.concatenate([p[:rows] for p in pieces], axis=2)
    other = across(jnp.concatenate([p[rows:] for p in pieces], axis=2), 1)
    lower = jnp.where(core == 0, own, other)
    upper = jnp.where(core == 0, other, own)
    rdm = jnp.stack([lower, upper], axis=2).reshape(rows, pair_cols)
    return rdm, grad


def solution(mesh):
    secs, gens = mesh.shape["sec"], mesh.shape["gen"]
    placed = (
        P("sec", "gen", None),
        P("sec", "gen", None),
        P("sec"),
        P("gen", None, "sec"),
        P("gen", None),
    )
    def step(*args):
        rows, general, width = args[0].shape[1], args[3].shape[0], args[3].shape[1]
        fits = secs == 4 and gens == 8 and 2 * general == width and rows == 128 * CHUNKS
        return (shards if fits else general_shards)(secs, gens, *args)

    return jax.shard_map(
        step,
        mesh=mesh,
        in_specs=placed,
        out_specs=(P("gen", "sec"), P("gen", None)),
        check_vma=False,
    )
```

```python
import functools

import jax
import jax.numpy as jnp
from jax import lax
from jax.experimental import pallas as pl
from jax.experimental.pallas import tpu as pltpu
from jax.sharding import PartitionSpec as P

CHUNKS = 4
GROUPS = ((0,), (1,), (2,), (3,))
ORDER = (
    "W0", "M0", "W1", "A1", "P0", "M1", "W2", "A2", "P1", "M2", "C0", "W3", "A3", "M3",
    "P2", "C1", "F0", "P3", "C2", "F1", "F2", "C3", "R", "F3",
)
LIMIT = 50 * 2**20
NT = (((1,), (1,)), ((), ()))
HBM = pl.BlockSpec(memory_space=pltpu.HBM)
VMEM = pl.BlockSpec(memory_space=pltpu.VMEM)
SMEM = pl.BlockSpec(memory_space=pltpu.SMEM)
PARAMS = pltpu.CompilerParams(vmem_limit_bytes=LIMIT)


def cost(flops):
    return pl.CostEstimate(flops=flops, bytes_accessed=1, transcendentals=0)


def partial_kernel(cuts, nears, info, left, partner, *refs):
    own, far, bra, ket, bra_sem, ket_sem = refs[-6:]
    pieces, near = refs[: -6 - nears], refs[-6 - nears : -6]
    sectors, rows, states = left.shape
    cols = own.shape[2]
    copies = []
    for n, (ref, index, start, r) in enumerate(cuts):
        piece = pieces[ref].at[index]
        at = pl.multiple_of((info[0] ^ r) * cols + start, 16)
        copies.append(pltpu.make_async_copy(piece, bra.at[:, pl.ds(at, piece.shape[1])], bra_sem.at[n]))
    kets = [
        pltpu.make_async_copy(ref, ket.at[c], ket_sem.at[c]) for c, ref in enumerate((left, partner))
    ]
    for copy in copies + kets:
        copy.start()
    for copy in copies:
        copy.wait()
    ids = lax.broadcasted_iota(jnp.int32, (rows, states), 1)
    for c in range(2):
        kets[c].wait()
        out = None
        for s in range(sectors):
            live = jnp.where(ids < info[1 + s], ket[c, s].astype(jnp.float32), 0.0)
            term = lax.dot_general(
                live.astype(jnp.bfloat16), bra[s], NT, preferred_element_type=jnp.float32
            )
            out = term if out is None else out + term
        blocks = [out[:, k * cols : (k + 1) * cols] for k in range(4)]
        own[c] = blocks[0]
        near[0][0, c] = blocks[1].astype(jnp.bfloat16)
        near[nears - 1][2 - nears, c] = blocks[3].astype(jnp.bfloat16)
        far[c] = blocks[2].astype(far.dtype)


def partial_products(info, left, partner, cols, cuts, nears, *pieces):
    sectors, rows, states = left.shape

    block = (2, rows, cols)
    return pl.pallas_call(
        functools.partial(partial_kernel, cuts, nears),
        in_specs=[SMEM] + [HBM] * (2 + len(pieces)),
        out_specs=[VMEM] * (nears + 2),
        scratch_shapes=[
            pltpu.VMEM((sectors, 4 * cols, states), jnp.bfloat16),
            pltpu.VMEM((2, sectors, rows, states), jnp.bfloat16),
            pltpu.SemaphoreType.DMA((len(cuts),)),
            pltpu.SemaphoreType.DMA((2,)),
        ],
        out_shape=[
            jax.ShapeDtypeStruct((2 // nears, *block), jnp.bfloat16),
        ]
        * nears
        + [jax.ShapeDtypeStruct(block, jnp.float32)] * 2,
        compiler_params=PARAMS,
        cost_estimate=cost(16 * rows * sectors * states * cols),
        name="partial_products",
    )(info, left, partner, *pieces)


def combine_kernel(chunk, position, core, mine, a, b, *refs):
    rdm, others, turned, own, other, block, sems = refs[-7:]
    rows, cols = own.shape
    f32 = jnp.float32
    total = (mine[...] + a[0].astype(f32)) + b[...].astype(f32)
    own[...] = total[0].astype(jnp.bfloat16)
    other[...] = total[1].astype(jnp.bfloat16)
    at = pl.multiple_of(core[0] * rows + chunk * cols, 128)
    copies = [
        pltpu.make_async_copy(own, rdm.at[:, pl.ds(at, cols)], sems.at[0]),
        pltpu.make_async_copy(other, others.at[:, pl.ds(chunk * cols, cols)], sems.at[1]),
        pltpu.make_async_copy(block, turned.at[position], sems.at[2]),
    ]
    for copy in copies[:2]:
        copy.start()
    width = block.shape[0]
    by_row = total.reshape(2 * rows // width, width, cols)
    block[...] = jnp.swapaxes(by_row, 0, 1).astype(jnp.bfloat16)
    copies[2].start()
    for copy in copies:
        copy.wait()


def combine(chunk, group, core, mine, near, far, width, pair_cols, held):
    _, rows, cols = mine.shape
    bf16 = jnp.bfloat16
    block = (width, 2 * rows // width, cols)
    return pl.pallas_call(
        functools.partial(combine_kernel, chunk, group.index(chunk)),
        in_specs=[SMEM] + [VMEM] * 3 + [HBM] * len(held),
        out_specs=[HBM] * 3,
        out_shape=[
            jax.ShapeDtypeStruct((rows, pair_cols), bf16),
            jax.ShapeDtypeStruct((rows, pair_cols // 2), bf16),
            jax.ShapeDtypeStruct((len(group), *block), bf16),
        ],
        scratch_shapes=[pltpu.VMEM((rows, cols), bf16)] * 2
        + [pltpu.VMEM(block, bf16), pltpu.SemaphoreType.DMA((3,))],
        input_output_aliases={4 + i: i for i in range(len(held))},
        compiler_params=PARAMS,
        cost_estimate=cost(8 * rows * cols),
        name="combine",
    )(core, mine, near, far, *held)


def place_kernel(core, other, held, rdm, sem):
    rows = other.shape[1]
    at = pl.multiple_of((1 - core[0]) * rows, 128)
    copy = pltpu.make_async_copy(other, rdm.at[:, pl.ds(at, rows)], sem)
    copy.start()
    copy.wait()


def place(core, other, rdm):
    return pl.pallas_call(
        place_kernel,
        in_specs=[SMEM, VMEM, HBM],
        out_specs=HBM,
        out_shape=jax.ShapeDtypeStruct(rdm.shape, rdm.dtype),
        scratch_shapes=[pltpu.SemaphoreType.DMA],
        input_output_aliases={2: 0},
        compiler_params=PARAMS,
        name="place",
    )(core, other, rdm)


def fock_kernel(first, base, slab, diagonal, *refs):
    *pieces, fock, traced, part, rdm, sems = refs
    width, orbitals, total = part.shape
    chunks, _, _, cols = pieces[0].shape
    copies = [pltpu.make_async_copy(slab.at[:, :, pl.ds(first * cols, total)], part, sems.at[4])]
    for r in range(4):
        piece = pieces[r] if len(pieces) == 4 else pieces[min(r, 2)]
        if len(pieces) == 3 and r >= 2:
            piece = piece.at[pl.ds((r - 2) * chunks, chunks)]
        copies.append(pltpu.make_async_copy(piece, rdm.at[base[0] ^ r], sems.at[r]))
    for copy in copies:
        copy.start()
    for copy in copies:
        copy.wait()
    acc = jnp.zeros((orbitals, width), jnp.float32)
    for u in range(width):
        trace = None
        for n in range(chunks):
            at = slice(n * cols, (n + 1) * cols)
            lhs = jnp.concatenate([part[u, :, at], diagonal[:, at]], axis=0)
            rhs = jnp.concatenate([rdm[c, n, u] for c in range(4)], axis=0)
            out = lax.dot_general(lhs, rhs, NT, preferred_element_type=jnp.float32)
            acc += out[:orbitals]
            trace = out[orbitals] if trace is None else trace + out[orbitals]
        traced[u, :] = trace
    fock[...] = acc


def fock_terms(first, base, slab, diagonal, *pieces):
    width, orbitals, _ = slab.shape
    chunks, _, _, cols = pieces[0].shape
    return pl.pallas_call(
        functools.partial(fock_kernel, first),
        in_specs=[SMEM, HBM, VMEM] + [HBM] * len(pieces),
        out_specs=[VMEM] * 2,
        out_shape=[
            jax.ShapeDtypeStruct((orbitals, width), jnp.float32),
            jax.ShapeDtypeStruct((width, width), jnp.float32),
        ],
        scratch_shapes=[
            pltpu.VMEM((width, orbitals, chunks * cols), jnp.bfloat16),
            pltpu.VMEM((4, *pieces[0].shape), jnp.bfloat16),
            pltpu.SemaphoreType.DMA((5,)),
        ],
        compiler_params=PARAMS,
        cost_estimate=cost(2 * (orbitals + 16) * width * width * chunks * cols),
        name="fock_terms",
    )(base, slab, diagonal, *pieces)


def turn_kernel(core, a, b, o):
    size = a.shape[0]
    o[:, :size] = jnp.swapaxes(a[...].astype(jnp.float32), 0, 1).astype(jnp.bfloat16)
    o[:, size:] = jnp.swapaxes(b[...].astype(jnp.float32), 0, 1).astype(jnp.bfloat16)


def turn(core, slab, received, cols):
    orbitals, width, total = received.shape
    steps = total // cols
    return pl.pallas_call(
        turn_kernel,
        grid_spec=pltpu.PrefetchScalarGridSpec(
            num_scalar_prefetch=1,
            grid=(steps,),
            in_specs=[
                pl.BlockSpec((orbitals, width, cols), lambda i, core: (0, 0, core[0] * steps + i)),
                pl.BlockSpec((orbitals, width, cols), lambda i, core: (0, 0, i)),
            ],
            out_specs=pl.BlockSpec((width, 2 * orbitals, cols), lambda i, core: (0, 0, i)),
        ),
        out_shape=jax.ShapeDtypeStruct((width, 2 * orbitals, total), jnp.bfloat16),
        compiler_params=PARAMS,
        cost_estimate=cost(orbitals * width * total),
        name="turn",
    )(core, slab, received)


def after(value, *done):
    done = jax.tree.leaves(done)
    return lax.optimization_barrier((value, *done))[0]


def shards(secs, gens, amps_left, amps_right, block_sizes, slab, fcore):
    sectors, rows, states = amps_left.shape
    general, width, pair_cols = slab.shape
    cols = rows // CHUNKS
    half = cols // 2
    z = lax.axis_index("sec")
    g = lax.axis_index("gen")
    chip, core = g // 2, g % 2

    def across(value, flip):
        return lax.ppermute(value, "gen", [(i, i ^ flip) for i in range(gens)])

    def along(value, flip):
        return lax.ppermute(value, "sec", [(i, i ^ flip) for i in range(secs)])

    def number(value):
        return value.reshape(1).astype(jnp.int32)

    def bra(chunk, source):
        return source[:, chunk * cols : (chunk + 1) * cols]

    sent = bra(0, amps_right)
    pieces = {}
    if ORDER[0] == "W0":
        xs, ys = across(sent, 2), across(sent, 4)
    else:
        pieces[0] = [across(sent, 2 * r) for r in (1, 2, 3)]
    partner_left = across(amps_left, 1)
    later = after(amps_right, sent)
    waiting = [None] + [bra(chunk, later) for chunk in range(1, CHUNKS)]

    given = lax.dynamic_slice(after(slab, sent), (0, 0, (1 - core) * rows), (general, width, rows))
    received, *waiting[1:] = lax.optimization_barrier((across(given, 1), *waiting[1:]))
    integrals = turn(number(core), slab, received, cols)

    column_ids = z * pair_cols + core * rows + jnp.arange(rows, dtype=jnp.int32)
    diagonal = jnp.broadcast_to(
        (column_ids // width == column_ids % width).astype(jnp.bfloat16)[None], (16, rows)
    )

    def products(chunk, nears, *parts):
        mine = slice(chunk * cols, (chunk + 1) * cols)
        every = slice(None)
        cuts = [(0, (every, mine), 0, 0)] + [(n, (every,), 0, n) for n in range(1, 4)]
        if len(parts) == 4:
            cuts.append((4, (every,), half, 3))
        info = jnp.concatenate([number(chip ^ z), block_sizes])
        return partial_products(info, amps_left, partner_left, cols, cuts, nears, amps_right, *parts)

    sums, terms, gathered = [None] * CHUNKS, [], {}

    def contract(group):
        at = slice(group[0] * cols, (group[-1] + 1) * cols)
        marks = after(diagonal[:, at], state["last"])
        terms.append(fock_terms(group[0], number(chip), integrals, marks, *gathered[group]))
        state["last"] = terms[-1][0]

    if 0 in pieces:
        state = {"last": (), "held": ()}
        sent = after(waiting[1], *pieces[0], integrals)
        state["xs"], state["ys"] = across(sent, 2), across(sent, 4)
    else:
        state = {"last": integrals, "held": (), "xs": xs, "ys": ys}

    def do_forward(chunk):
        last = state["last"]
        xs, ys = after(state["xs"], last), after(state["ys"], last)
        lower, upper = xs[:, :half], ys[:, half:]
        pieces[chunk] = (xs, ys, across(lower, 4), across(upper, 2))
        state["last"] = (lower, upper)
        if chunk + 1 < CHUNKS:
            sent = after(waiting[chunk + 1], xs, ys)
            state["xs"], state["ys"] = across(sent, 2), across(sent, 4)

    def do_products(chunk):
        nears = 2 if chunk == CHUNKS - 1 else 1
        *near, own, far = products(chunk, nears, *(after(p, state["last"]) for p in pieces[chunk]))
        near[-1] = along(near[-1], 1)
        sums[chunk] = [own, near, far]
        state["last"] = own

    def do_pass(chunk):
        own, near, far = sums[chunk]
        far = after(far, state["last"])
        passed = (far + near[-1][-1].astype(jnp.float32)).astype(jnp.bfloat16)
        if len(near) == 2:
            near[0] = along(after(near[0], passed), 1)
        sums[chunk] = [own, near[0], along(passed, 2)]
        state["last"] = passed

    def do_finish(chunk):
        own, near, far = sums[chunk]
        group = [g for g in GROUPS if chunk in g][0]
        held = state["held"] if chunk > group[0] else state["held"][:2]
        state["held"] = combine(
            chunk, group, number(core), after(own, state["last"]), near, far, width, pair_cols, held
        )
        turned = state["held"][2]
        if chunk == group[-1]:
            if True:
                gathered[group] = (turned, *[across(turned, 2 * r) for r in (1, 2, 3)])
            else:
                gathered[group] = (turned, across(turned, 2))
        state["last"] = state["held"][1]

    def do_second(chunk):
        group = [g for g in GROUPS if chunk in g][0]
        both = jnp.concatenate([after(p, state["last"]) for p in gathered[group]], axis=0)
        gathered[group] += (across(both, 4),)
        state["last"] = both

    def do_wait(chunk):
        state["last"] = (state["last"], *pieces[chunk][2:])

    steps = {
        "W": do_forward,
        "A": do_wait,
        "M": do_products,
        "P": do_pass,
        "C": do_finish,
        "H": do_second,
        "F": lambda chunk: contract([g for g in GROUPS if chunk in g][0]),
    }
    for step in ORDER:
        if step == "R":
            rdm = place(number(core), across(state["held"][1], 1), state["held"][0])
            state["last"] = rdm
        else:
            steps[step[0]](int(step[1]))

    two_body = sum(t[0] for t in terms)
    traced = sum(t[1] for t in terms)

    def ordered(value):
        split = value.reshape(value.shape[0], 4, 2, -1)
        return jnp.where(core == 0, split, split[:, :, ::-1]).reshape(value.shape)

    one = ordered(traced).T / width
    both = jnp.concatenate([fcore, across(fcore, 1)], axis=0).astype(jnp.float32)
    mine = ordered(two_body) + jnp.dot(both, one, precision=lax.Precision.HIGHEST)
    theirs = across(mine, 1)
    fock = mine[:general] + theirs[general:]
    partner = mine[general:] + theirs[:general]

    first = jnp.where(core == 0, fock, partner)
    second = jnp.where(core == 0, partner, fock)
    active = jnp.concatenate([first, second], axis=0)
    flipped = lax.dynamic_slice_in_dim(active.T, core * general, general, axis=0)
    part = 2.0 * (fock - jnp.where(g < 2, flipped, 0.0))
    for flip in (1, 2):
        part = part + along(part, flip)
    return rdm, part


def general_shards(secs, gens, amps_left, amps_right, block_sizes, slab, fcore):
    sectors, rows, states = amps_left.shape
    general, width, pair_cols = slab.shape
    chips = gens // 2
    per_sec = chips // secs
    bits = chips.bit_length() - 1
    chunks = 1
    half = rows // chunks // 2
    z = lax.axis_index("sec")
    g = lax.axis_index("gen")
    chip, core = g // 2, g % 2

    def across(value, flip):
        return lax.ppermute(value, "gen", [(i, i ^ flip) for i in range(gens)])

    def along(value, flip):
        return lax.ppermute(value, "sec", [(i, i ^ flip) for i in range(secs)])

    def gather(value, order):
        held = value[None]
        for bit in order:
            held = jnp.concatenate([held, across(held, 2 << bit)], axis=0)
        return held

    def place(relative, order):
        return sum(((relative >> bit) & 1) << at for at, bit in enumerate(order))

    orders = (tuple(range(bits)), tuple(reversed(range(bits))))
    live = (jnp.arange(states, dtype=jnp.int32)[None, :] < block_sizes[:, None]).astype(jnp.bfloat16)

    left = jnp.concatenate([amps_left, across(amps_left, 1)], axis=1) * live[:, None, :]

    by_core = slab.reshape(general, width, per_sec, 2, rows)
    kept = lax.dynamic_index_in_dim(by_core, core, 3, keepdims=False)
    given = lax.dynamic_index_in_dim(by_core, 1 - core, 3, keepdims=False)
    integrals = jnp.concatenate([kept, across(given, 1)], axis=0)

    column_ids = (
        z * pair_cols
        + jnp.arange(per_sec, dtype=jnp.int32)[:, None] * (2 * rows)
        + core * rows
        + jnp.arange(rows, dtype=jnp.int32)[None, :]
    )
    diagonal = (column_ids // width == column_ids % width).astype(jnp.bfloat16)

    pieces = []
    two_body = jnp.zeros((2 * general, width), jnp.float32)
    traced = jnp.zeros((width, width), jnp.float32)
    for chunk in range(chunks):
        start = chunk * 2 * half
        blocks = [
            gather(amps_right[:, start + i * half : start + (i + 1) * half], orders[i])
            for i in range(2)
        ]

        def partial_for(dest):
            wanted = chip ^ (dest * per_sec + jnp.arange(per_sec, dtype=jnp.int32))
            found = [
                jnp.take(blocks[i], place(wanted, orders[i]), axis=0) for i in range(2)
            ]
            right = jnp.concatenate(found, axis=2)
            return jnp.einsum(
                "srm,csqm->rcq", left, right, preferred_element_type=jnp.float32
            )

        arrived = [
            along(partial_for(z ^ flip).astype(jnp.bfloat16), flip) for flip in range(1, secs)
        ]
        total = partial_for(z)
        for value in arrived:
            total = total + value.astype(jnp.float32)
        piece = total.astype(jnp.bfloat16)
        pieces.append(piece)

        columns = per_sec * 2 * half
        by_row = piece.reshape(2, rows // width, width, columns)
        halves = [gather(by_row[i], orders[i]) for i in range(2)]
        table = jnp.arange(chips, dtype=jnp.int32)
        halves[1] = halves[1][jnp.array([sum(((p >> b) & 1) << a for a, b in enumerate(orders[1])) for p in range(chips)])]
        every = jnp.stack(halves, axis=1).reshape(width, width, columns)
        part = integrals[:, :, :, start : start + 2 * half].reshape(2 * general, width, columns)
        two_body = two_body + jnp.einsum(
            "puq,tuq->pt", part, every, preferred_element_type=jnp.float32
        )
        traced = traced + jnp.einsum(
            "tuq,q->tu",
            every,
            diagonal[:, start : start + 2 * half].reshape(columns),
            preferred_element_type=jnp.float32,
        )

    def ordered(value, axis):
        shape = value.shape
        split = value.reshape(shape[:axis] + (gens, shape[axis] // gens) + shape[axis + 1 :])
        return jnp.take(split, g ^ jnp.arange(gens), axis=axis).reshape(shape)

    two_body = ordered(two_body, 1)
    one = ordered(traced, 0) / width
    both = jnp.concatenate([fcore, across(fcore, 1)], axis=0).astype(jnp.float32)
    mine = two_body + jnp.dot(both, one, precision=lax.Precision.HIGHEST)
    theirs = across(mine, 1)
    fock = mine[:general] + theirs[general:]
    partner = mine[general:] + theirs[:general]

    first = jnp.where(core == 0, fock, partner)
    second = jnp.where(core == 0, partner, fock)
    active = jnp.concatenate([first, second], axis=0)
    flipped = lax.dynamic_slice_in_dim(active.T, core * general, general, axis=0)
    part = 2.0 * (fock - jnp.where(g < 2, flipped, 0.0))
    parts = [part] + [along(part, flip) for flip in range(1, secs)]
    while len(parts) > 1:
        parts = [a + b for a, b in zip(parts[::2], parts[1::2])]
    grad = parts[0]

    own = jnp.concatenate([p[:rows] for p in pieces], axis=2)
    other = across(jnp.concatenate([p[rows:] for p in pieces], axis=2), 1)
    lower = jnp.where(core == 0, own, other)
    upper = jnp.where(core == 0, other, own)
    rdm = jnp.stack([lower, upper], axis=2).reshape(rows, pair_cols)
    return rdm, grad


def solution(mesh):
    secs, gens = mesh.shape["sec"], mesh.shape["gen"]
    placed = (
        P("sec", "gen", None),
        P("sec", "gen", None),
        P("sec"),
        P("gen", None, "sec"),
        P("gen", None),
    )
    def step(*args):
        rows, general, width = args[0].shape[1], args[3].shape[0], args[3].shape[1]
        fits = secs == 4 and gens == 8 and 2 * general == width and rows == 128 * CHUNKS
        return (shards if fits else general_shards)(secs, gens, *args)

    return jax.shard_map(
        step,
        mesh=mesh,
        in_specs=placed,
        out_specs=(P("gen", "sec"), P("gen", None)),
        check_vma=False,
    )
```

```python
import functools

import jax
import jax.numpy as jnp
from jax import lax
from jax.experimental import pallas as pl
from jax.experimental.pallas import tpu as pltpu
from jax.sharding import PartitionSpec as P

CHUNKS = 4
GROUPS = ((0,), (1,), (2,), (3,))
ORDER = (
    "W0", "M0", "W1", "A1", "P0", "M1", "W2", "A2", "P1", "M2", "C0", "W3", "A3", "M3", "P2", "C1", "F0", "P3", "C2", "F1", "F2", "C3", "R", "F3",
)
LIMIT = 50 * 2**20
WEIGHTS = {"M": (2000000000, 2000000000, 2000000000, 2000000000), "C": (1000000, 1000000, 1000000, 1000000), "F": (100000000, 100000000, 100000000, 2000000000), "T": 1000000}
NT = (((1,), (1,)), ((), ()))
HBM = pl.BlockSpec(memory_space=pltpu.HBM)
VMEM = pl.BlockSpec(memory_space=pltpu.VMEM)
SMEM = pl.BlockSpec(memory_space=pltpu.SMEM)
PARAMS = pltpu.CompilerParams(vmem_limit_bytes=LIMIT)


def cost(flops):
    return pl.CostEstimate(flops=flops, bytes_accessed=1, transcendentals=0)


def partial_kernel(cuts, nears, info, left, partner, *refs):
    own, far, bra, ket, bra_sem, ket_sem = refs[-6:]
    pieces, near = refs[: -6 - nears], refs[-6 - nears : -6]
    sectors, rows, states = left.shape
    cols = own.shape[2]
    copies = []
    for n, (ref, index, start, r) in enumerate(cuts):
        piece = pieces[ref].at[index]
        at = pl.multiple_of((info[0] ^ r) * cols + start, 16)
        copies.append(pltpu.make_async_copy(piece, bra.at[:, pl.ds(at, piece.shape[1])], bra_sem.at[n]))
    kets = [
        pltpu.make_async_copy(ref, ket.at[c], ket_sem.at[c]) for c, ref in enumerate((left, partner))
    ]
    for copy in copies + kets:
        copy.start()
    for copy in copies:
        copy.wait()
    ids = lax.broadcasted_iota(jnp.int32, (rows, states), 1)
    for c in range(2):
        kets[c].wait()
        out = None
        for s in range(sectors):
            live = jnp.where(ids < info[1 + s], ket[c, s].astype(jnp.float32), 0.0)
            term = lax.dot_general(
                live.astype(jnp.bfloat16), bra[s], NT, preferred_element_type=jnp.float32
            )
            out = term if out is None else out + term
        blocks = [out[:, k * cols : (k + 1) * cols] for k in range(4)]
        own[c] = blocks[0]
        near[0][0, c] = blocks[1].astype(jnp.bfloat16)
        near[nears - 1][2 - nears, c] = blocks[3].astype(jnp.bfloat16)
        far[c] = blocks[2].astype(far.dtype)


def partial_products(weight, info, left, partner, cols, cuts, nears, *pieces):
    sectors, rows, states = left.shape

    block = (2, rows, cols)
    return pl.pallas_call(
        functools.partial(partial_kernel, cuts, nears),
        in_specs=[SMEM] + [HBM] * (2 + len(pieces)),
        out_specs=[VMEM] * (nears + 2),
        scratch_shapes=[
            pltpu.VMEM((sectors, 4 * cols, states), jnp.bfloat16),
            pltpu.VMEM((2, sectors, rows, states), jnp.bfloat16),
            pltpu.SemaphoreType.DMA((len(cuts),)),
            pltpu.SemaphoreType.DMA((2,)),
        ],
        out_shape=[
            jax.ShapeDtypeStruct((2 // nears, *block), jnp.bfloat16),
        ]
        * nears
        + [jax.ShapeDtypeStruct(block, jnp.float32)] * 2,
        compiler_params=PARAMS,
        cost_estimate=cost(weight),
        name="partial_products",
    )(info, left, partner, *pieces)


def combine_kernel(chunk, position, core, mine, a, b, *refs):
    rdm, others, turned, own, other, block, sems = refs[-7:]
    rows, cols = own.shape
    f32 = jnp.float32
    total = (mine[...] + a[0].astype(f32)) + b[...].astype(f32)
    own[...] = total[0].astype(jnp.bfloat16)
    other[...] = total[1].astype(jnp.bfloat16)
    at = pl.multiple_of(core[0] * rows + chunk * cols, 128)
    copies = [
        pltpu.make_async_copy(own, rdm.at[:, pl.ds(at, cols)], sems.at[0]),
        pltpu.make_async_copy(other, others.at[:, pl.ds(chunk * cols, cols)], sems.at[1]),
        pltpu.make_async_copy(block, turned.at[position], sems.at[2]),
    ]
    for copy in copies[:2]:
        copy.start()
    width = block.shape[0]
    by_row = total.reshape(2 * rows // width, width, cols)
    block[...] = jnp.swapaxes(by_row, 0, 1).astype(jnp.bfloat16)
    copies[2].start()
    for copy in copies:
        copy.wait()


def combine(weight, chunk, group, core, mine, near, far, width, pair_cols, held):
    _, rows, cols = mine.shape
    bf16 = jnp.bfloat16
    block = (width, 2 * rows // width, cols)
    return pl.pallas_call(
        functools.partial(combine_kernel, chunk, group.index(chunk)),
        in_specs=[SMEM] + [VMEM] * 3 + [HBM] * len(held),
        out_specs=[HBM] * 3,
        out_shape=[
            jax.ShapeDtypeStruct((rows, pair_cols), bf16),
            jax.ShapeDtypeStruct((rows, pair_cols // 2), bf16),
            jax.ShapeDtypeStruct((len(group), *block), bf16),
        ],
        scratch_shapes=[pltpu.VMEM((rows, cols), bf16)] * 2
        + [pltpu.VMEM(block, bf16), pltpu.SemaphoreType.DMA((3,))],
        input_output_aliases={4 + i: i for i in range(len(held))},
        compiler_params=PARAMS,
        cost_estimate=cost(weight),
        name="combine",
    )(core, mine, near, far, *held)


def place_kernel(core, other, held, rdm, sem):
    rows = other.shape[1]
    at = pl.multiple_of((1 - core[0]) * rows, 128)
    copy = pltpu.make_async_copy(other, rdm.at[:, pl.ds(at, rows)], sem)
    copy.start()
    copy.wait()


def place(core, other, rdm):
    return pl.pallas_call(
        place_kernel,
        in_specs=[SMEM, VMEM, HBM],
        out_specs=HBM,
        out_shape=jax.ShapeDtypeStruct(rdm.shape, rdm.dtype),
        scratch_shapes=[pltpu.SemaphoreType.DMA],
        input_output_aliases={2: 0},
        compiler_params=PARAMS,
        name="place",
    )(core, other, rdm)


def fock_kernel(first, base, slab, diagonal, *refs):
    *pieces, fock, traced, part, rdm, sems = refs
    width, orbitals, total = part.shape
    chunks, _, _, cols = pieces[0].shape
    copies = [pltpu.make_async_copy(slab.at[:, :, pl.ds(first * cols, total)], part, sems.at[4])]
    for r in range(4):
        piece = pieces[r] if len(pieces) == 4 else pieces[min(r, 2)]
        if len(pieces) == 3 and r >= 2:
            piece = piece.at[pl.ds((r - 2) * chunks, chunks)]
        copies.append(pltpu.make_async_copy(piece, rdm.at[base[0] ^ r], sems.at[r]))
    for copy in copies:
        copy.start()
    for copy in copies:
        copy.wait()
    acc = jnp.zeros((orbitals, width), jnp.float32)
    for u in range(width):
        trace = None
        for n in range(chunks):
            at = slice(n * cols, (n + 1) * cols)
            lhs = jnp.concatenate([part[u, :, at], diagonal[:, at]], axis=0)
            rhs = jnp.concatenate([rdm[c, n, u] for c in range(4)], axis=0)
            out = lax.dot_general(lhs, rhs, NT, preferred_element_type=jnp.float32)
            acc += out[:orbitals]
            trace = out[orbitals] if trace is None else trace + out[orbitals]
        traced[u, :] = trace
    fock[...] = acc


def fock_terms(weight, first, base, slab, diagonal, *pieces):
    width, orbitals, _ = slab.shape
    chunks, _, _, cols = pieces[0].shape
    return pl.pallas_call(
        functools.partial(fock_kernel, first),
        in_specs=[SMEM, HBM, VMEM] + [HBM] * len(pieces),
        out_specs=[VMEM] * 2,
        out_shape=[
            jax.ShapeDtypeStruct((orbitals, width), jnp.float32),
            jax.ShapeDtypeStruct((width, width), jnp.float32),
        ],
        scratch_shapes=[
            pltpu.VMEM((width, orbitals, chunks * cols), jnp.bfloat16),
            pltpu.VMEM((4, *pieces[0].shape), jnp.bfloat16),
            pltpu.SemaphoreType.DMA((5,)),
        ],
        compiler_params=PARAMS,
        cost_estimate=cost(weight),
        name="fock_terms",
    )(base, slab, diagonal, *pieces)


def turn_kernel(core, a, b, o):
    size = a.shape[0]
    o[:, :size] = jnp.swapaxes(a[...].astype(jnp.float32), 0, 1).astype(jnp.bfloat16)
    o[:, size:] = jnp.swapaxes(b[...].astype(jnp.float32), 0, 1).astype(jnp.bfloat16)


def turn(weight, core, slab, received, cols):
    orbitals, width, total = received.shape
    steps = total // cols
    return pl.pallas_call(
        turn_kernel,
        grid_spec=pltpu.PrefetchScalarGridSpec(
            num_scalar_prefetch=1,
            grid=(steps,),
            in_specs=[
                pl.BlockSpec((orbitals, width, cols), lambda i, core: (0, 0, core[0] * steps + i)),
                pl.BlockSpec((orbitals, width, cols), lambda i, core: (0, 0, i)),
            ],
            out_specs=pl.BlockSpec((width, 2 * orbitals, cols), lambda i, core: (0, 0, i)),
        ),
        out_shape=jax.ShapeDtypeStruct((width, 2 * orbitals, total), jnp.bfloat16),
        compiler_params=PARAMS,
        cost_estimate=cost(weight),
        name="turn",
    )(core, slab, received)


def after(value, *done):
    done = jax.tree.leaves(done)
    return lax.optimization_barrier((value, *done))[0]


def shards(secs, gens, amps_left, amps_right, block_sizes, slab, fcore):
    sectors, rows, states = amps_left.shape
    general, width, pair_cols = slab.shape
    cols = rows // CHUNKS
    half = cols // 2
    z = lax.axis_index("sec")
    g = lax.axis_index("gen")
    chip, core = g // 2, g % 2

    def across(value, flip):
        return lax.ppermute(value, "gen", [(i, i ^ flip) for i in range(gens)])

    def along(value, flip):
        return lax.ppermute(value, "sec", [(i, i ^ flip) for i in range(secs)])

    def number(value):
        return value.reshape(1).astype(jnp.int32)

    def bra(chunk, source):
        return source[:, chunk * cols : (chunk + 1) * cols]

    sent = bra(0, amps_right)
    pieces = {}
    if ORDER[0] == "W0":
        xs, ys = across(sent, 2), across(sent, 4)
    else:
        pieces[0] = [across(sent, 2 * r) for r in (1, 2, 3)]
    partner_left = across(amps_left, 1)
    later = after(amps_right, sent)
    waiting = [None] + [bra(chunk, later) for chunk in range(1, CHUNKS)]

    given = lax.dynamic_slice(after(slab, sent), (0, 0, (1 - core) * rows), (general, width, rows))
    received, *waiting[1:] = lax.optimization_barrier((across(given, 1), *waiting[1:]))
    integrals = turn(WEIGHTS["T"], number(core), slab, received, cols)

    column_ids = z * pair_cols + core * rows + jnp.arange(rows, dtype=jnp.int32)
    diagonal = jnp.broadcast_to(
        (column_ids // width == column_ids % width).astype(jnp.bfloat16)[None], (16, rows)
    )

    def products(chunk, nears, *parts):
        mine = slice(chunk * cols, (chunk + 1) * cols)
        every = slice(None)
        cuts = [(0, (every, mine), 0, 0)] + [(n, (every,), 0, n) for n in range(1, 4)]
        if len(parts) == 4:
            cuts.append((4, (every,), half, 3))
        info = jnp.concatenate([number(chip ^ z), block_sizes])
        return partial_products(WEIGHTS["M"][chunk], info, amps_left, partner_left, cols, cuts, nears, amps_right, *parts)

    sums, terms, gathered = [None] * CHUNKS, [], {}

    def contract(group):
        at = slice(group[0] * cols, (group[-1] + 1) * cols)
        marks = after(diagonal[:, at], state["last"])
        terms.append(fock_terms(WEIGHTS["F"][group[0]], group[0], number(chip), integrals, marks, *gathered[group]))
        state["last"] = terms[-1][0]

    if 0 in pieces:
        state = {"last": (), "held": ()}
        sent = after(waiting[1], *pieces[0], integrals)
        state["xs"], state["ys"] = across(sent, 2), across(sent, 4)
    else:
        state = {"last": integrals, "held": (), "xs": xs, "ys": ys}

    def do_forward(chunk):
        last = state["last"]
        xs, ys = after(state["xs"], last), after(state["ys"], last)
        lower, upper = xs[:, :half], ys[:, half:]
        pieces[chunk] = (xs, ys, across(lower, 4), across(upper, 2))
        state["last"] = (lower, upper)
        if chunk + 1 < CHUNKS:
            sent = after(waiting[chunk + 1], xs, ys)
            state["xs"], state["ys"] = across(sent, 2), across(sent, 4)

    def do_products(chunk):
        nears = 2 if chunk == CHUNKS - 1 else 1
        *near, own, far = products(chunk, nears, *(after(p, state["last"]) for p in pieces[chunk]))
        near[-1] = along(near[-1], 1)
        sums[chunk] = [own, near, far]
        state["last"] = own

    def do_pass(chunk):
        own, near, far = sums[chunk]
        far = after(far, state["last"])
        passed = (far + near[-1][-1].astype(jnp.float32)).astype(jnp.bfloat16)
        if len(near) == 2:
            near[0] = along(after(near[0], passed), 1)
        sums[chunk] = [own, near[0], along(passed, 2)]
        state["last"] = passed

    def do_finish(chunk):
        own, near, far = sums[chunk]
        group = [g for g in GROUPS if chunk in g][0]
        held = state["held"] if chunk > group[0] else state["held"][:2]
        state["held"] = combine(
            WEIGHTS["C"][chunk], chunk, group, number(core), after(own, state["last"]), near, far, width, pair_cols, held
        )
        turned = state["held"][2]
        if chunk == group[-1]:
            if True:
                gathered[group] = (turned, *[across(turned, 2 * r) for r in (1, 2, 3)])
            else:
                gathered[group] = (turned, across(turned, 2))
        state["last"] = state["held"][1]

    def do_second(chunk):
        group = [g for g in GROUPS if chunk in g][0]
        both = jnp.concatenate([after(p, state["last"]) for p in gathered[group]], axis=0)
        gathered[group] += (across(both, 4),)
        state["last"] = both

    def do_wait(chunk):
        state["last"] = (state["last"], *pieces[chunk][2:])

    steps = {
        "W": do_forward,
        "A": do_wait,
        "M": do_products,
        "P": do_pass,
        "C": do_finish,
        "H": do_second,
        "F": lambda chunk: contract([g for g in GROUPS if chunk in g][0]),
    }
    for step in ORDER:
        if step == "R":
            rdm = place(number(core), across(state["held"][1], 1), state["held"][0])
            state["last"] = rdm
        else:
            steps[step[0]](int(step[1]))

    two_body = sum(t[0] for t in terms)
    traced = sum(t[1] for t in terms)

    def ordered(value):
        split = value.reshape(value.shape[0], 4, 2, -1)
        return jnp.where(core == 0, split, split[:, :, ::-1]).reshape(value.shape)

    one = ordered(traced).T / width
    both = jnp.concatenate([fcore, across(fcore, 1)], axis=0).astype(jnp.float32)
    mine = ordered(two_body) + jnp.dot(both, one, precision=lax.Precision.HIGHEST)
    theirs = across(mine, 1)
    fock = mine[:general] + theirs[general:]
    partner = mine[general:] + theirs[:general]

    first = jnp.where(core == 0, fock, partner)
    second = jnp.where(core == 0, partner, fock)
    active = jnp.concatenate([first, second], axis=0)
    flipped = lax.dynamic_slice_in_dim(active.T, core * general, general, axis=0)
    part = 2.0 * (fock - jnp.where(g < 2, flipped, 0.0))
    for flip in (1, 2):
        part = part + along(part, flip)
    return rdm, part


def general_shards(secs, gens, amps_left, amps_right, block_sizes, slab, fcore):
    sectors, rows, states = amps_left.shape
    general, width, pair_cols = slab.shape
    chips = gens // 2
    per_sec = chips // secs
    bits = chips.bit_length() - 1
    chunks = 1
    half = rows // chunks // 2
    z = lax.axis_index("sec")
    g = lax.axis_index("gen")
    chip, core = g // 2, g % 2

    def across(value, flip):
        return lax.ppermute(value, "gen", [(i, i ^ flip) for i in range(gens)])

    def along(value, flip):
        return lax.ppermute(value, "sec", [(i, i ^ flip) for i in range(secs)])

    def gather(value, order):
        held = value[None]
        for bit in order:
            held = jnp.concatenate([held, across(held, 2 << bit)], axis=0)
        return held

    def place(relative, order):
        return sum(((relative >> bit) & 1) << at for at, bit in enumerate(order))

    orders = (tuple(range(bits)), tuple(reversed(range(bits))))
    live = (jnp.arange(states, dtype=jnp.int32)[None, :] < block_sizes[:, None]).astype(jnp.bfloat16)

    left = jnp.concatenate([amps_left, across(amps_left, 1)], axis=1) * live[:, None, :]

    by_core = slab.reshape(general, width, per_sec, 2, rows)
    kept = lax.dynamic_index_in_dim(by_core, core, 3, keepdims=False)
    given = lax.dynamic_index_in_dim(by_core, 1 - core, 3, keepdims=False)
    integrals = jnp.concatenate([kept, across(given, 1)], axis=0)

    column_ids = (
        z * pair_cols
        + jnp.arange(per_sec, dtype=jnp.int32)[:, None] * (2 * rows)
        + core * rows
        + jnp.arange(rows, dtype=jnp.int32)[None, :]
    )
    diagonal = (column_ids // width == column_ids % width).astype(jnp.bfloat16)

    pieces = []
    two_body = jnp.zeros((2 * general, width), jnp.float32)
    traced = jnp.zeros((width, width), jnp.float32)
    for chunk in range(chunks):
        start = chunk * 2 * half
        blocks = [
            gather(amps_right[:, start + i * half : start + (i + 1) * half], orders[i])
            for i in range(2)
        ]

        def partial_for(dest):
            wanted = chip ^ (dest * per_sec + jnp.arange(per_sec, dtype=jnp.int32))
            found = [
                jnp.take(blocks[i], place(wanted, orders[i]), axis=0) for i in range(2)
            ]
            right = jnp.concatenate(found, axis=2)
            return jnp.einsum(
                "srm,csqm->rcq", left, right, preferred_element_type=jnp.float32
            )

        arrived = [
            along(partial_for(z ^ flip).astype(jnp.bfloat16), flip) for flip in range(1, secs)
        ]
        total = partial_for(z)
        for value in arrived:
            total = total + value.astype(jnp.float32)
        piece = total.astype(jnp.bfloat16)
        pieces.append(piece)

        columns = per_sec * 2 * half
        by_row = piece.reshape(2, rows // width, width, columns)
        halves = [gather(by_row[i], orders[i]) for i in range(2)]
        table = jnp.arange(chips, dtype=jnp.int32)
        halves[1] = halves[1][jnp.array([sum(((p >> b) & 1) << a for a, b in enumerate(orders[1])) for p in range(chips)])]
        every = jnp.stack(halves, axis=1).reshape(width, width, columns)
        part = integrals[:, :, :, start : start + 2 * half].reshape(2 * general, width, columns)
        two_body = two_body + jnp.einsum(
            "puq,tuq->pt", part, every, preferred_element_type=jnp.float32
        )
        traced = traced + jnp.einsum(
            "tuq,q->tu",
            every,
            diagonal[:, start : start + 2 * half].reshape(columns),
            preferred_element_type=jnp.float32,
        )

    def ordered(value, axis):
        shape = value.shape
        split = value.reshape(shape[:axis] + (gens, shape[axis] // gens) + shape[axis + 1 :])
        return jnp.take(split, g ^ jnp.arange(gens), axis=axis).reshape(shape)

    two_body = ordered(two_body, 1)
    one = ordered(traced, 0) / width
    both = jnp.concatenate([fcore, across(fcore, 1)], axis=0).astype(jnp.float32)
    mine = two_body + jnp.dot(both, one, precision=lax.Precision.HIGHEST)
    theirs = across(mine, 1)
    fock = mine[:general] + theirs[general:]
    partner = mine[general:] + theirs[:general]

    first = jnp.where(core == 0, fock, partner)
    second = jnp.where(core == 0, partner, fock)
    active = jnp.concatenate([first, second], axis=0)
    flipped = lax.dynamic_slice_in_dim(active.T, core * general, general, axis=0)
    part = 2.0 * (fock - jnp.where(g < 2, flipped, 0.0))
    parts = [part] + [along(part, flip) for flip in range(1, secs)]
    while len(parts) > 1:
        parts = [a + b for a, b in zip(parts[::2], parts[1::2])]
    grad = parts[0]

    own = jnp.concatenate([p[:rows] for p in pieces], axis=2)
    other = across(jnp.concatenate([p[rows:] for p in pieces], axis=2), 1)
    lower = jnp.where(core == 0, own, other)
    upper = jnp.where(core == 0, other, own)
    rdm = jnp.stack([lower, upper], axis=2).reshape(rows, pair_cols)
    return rdm, grad


def solution(mesh):
    secs, gens = mesh.shape["sec"], mesh.shape["gen"]
    placed = (
        P("sec", "gen", None),
        P("sec", "gen", None),
        P("sec"),
        P("gen", None, "sec"),
        P("gen", None),
    )
    def step(*args):
        rows, general, width = args[0].shape[1], args[3].shape[0], args[3].shape[1]
        fits = secs == 4 and gens == 8 and 2 * general == width and rows == 128 * CHUNKS
        return (shards if fits else general_shards)(secs, gens, *args)

    return jax.shard_map(
        step,
        mesh=mesh,
        in_specs=placed,
        out_specs=(P("gen", "sec"), P("gen", None)),
        check_vma=False,
    )
```
